32 devices in a mesh: grp: 4 (over z), ep: 8 (over y, x, core).
Axes of the slice: x: 2, y: 2, z: 4, core: 2. Of those that a mesh axis runs over, the one named last changes fastest.
Arguments:
- tokens: bfloat16 [512, 4096], P('grp', 'ep'), may hold values from -6 to 6
- grad_out: bfloat16 [512, 4096], P('grp', 'ep'), may hold values from -1.5 to 1.5
- routes: int32 [512, 2], P('grp'), may hold values from 0 to 1, as said below
- route_weights: float32 [512, 2], P('grp'), may hold values from 0.1 to 1
- gate_weight: bfloat16 [4, 384, 4096], P('grp'), may hold values from -0.09375 to 0.09375
- up_weight: bfloat16 [4, 384, 4096], P('grp'), may hold values from -0.09375 to 0.09375
- down_weight: bfloat16 [4, 384, 4096], P('grp'), may hold values from -0.21875 to 0.21875
Outputs:
- grad_tokens: bfloat16 [512, 4096], P('grp', 'ep')
- grad_gates: float32 [512, 2], P('grp')
The draws below stay inside these ranges and needn't reach their ends.
Inputs may be any that keep to these rules, and one draw needn't show every extreme that they name: The 2 routes of a token name different experts. Among the routes of the 128 tokens of one group, no expert is named more than 128 times; in every draw one expert is named exactly 128 times in every group.
All inputs are finite; a program needn't handle non-finite values.
Results may differ from the reference program's by a relative error of at most 0.0065.
Values may be sent and summed in bfloat16 or wider, within the bound.
No kernel may reach another device: no remote copies, remote signals or barrier semaphores. Data moves between devices by JAX's collectives and lax.ppermute only.
A program may use at most 64 MiB of HBM per device.

```python
import math
import jax
import jax.numpy as jnp
from jax import lax

D = 4096
FF = 768
TOP = 2
HALF = 384
EXPERTS = 2
TOKG = 128
TOKENS = 512
CAP = 128
N_GRP = 4


def draw_routes(key, part):
    key_hot, key_groups = jax.random.split(key)
    hot_expert = jax.random.randint(key_hot, (), 0, EXPERTS).astype(jnp.int32)

    def one_group(group_key):
        sub_keys = jax.random.split(group_key, 5)
        others = jax.random.permutation(sub_keys[0], EXPERTS - 1).astype(jnp.int32) + 1
        ordering = (hot_expert + jnp.concatenate([jnp.zeros((1,), jnp.int32), others])) % EXPERTS
        offset_first = jax.random.randint(sub_keys[1], (), 0, EXPERTS - 1).astype(jnp.int32)
        offset_rest = jax.random.randint(sub_keys[2], (), 0, EXPERTS - 1).astype(jnp.int32)
        token_pos = jnp.arange(TOKG, dtype=jnp.int32)
        in_first = token_pos < CAP
        later_pos = 2 * (token_pos - CAP) + offset_rest
        lead_pos = jnp.where(in_first, 0, 1 + later_pos % (EXPERTS - 1))
        trail_pos = jnp.where(in_first, 1 + (token_pos + offset_first) % (EXPERTS - 1), 1 + (later_pos + 1) % (EXPERTS - 1))
        flipped = jax.random.randint(sub_keys[3], (TOKG,), 0, 2) == 1
        first_col = jnp.where(flipped, trail_pos, lead_pos)
        second_col = jnp.where(flipped, lead_pos, trail_pos)
        picked = ordering[jnp.stack([first_col, second_col], axis=1)]
        shuffle = jax.random.permutation(sub_keys[4], TOKG)
        return picked[shuffle]
    group_keys = jax.random.split(key_groups, TOKENS // TOKG)
    return jax.vmap(one_group)(group_keys).reshape(TOKENS, TOP).astype(jnp.int32)


def levels(key, extent, cuts, least, top_value):
    def one(dim, parts):
        draws = jax.random.uniform(jax.random.fold_in(jax.random.fold_in(key, 6), dim), (parts,), jnp.float32, least / len(cuts), top_value / len(cuts))
        return jnp.repeat(jnp.exp(draws), extent[dim] // parts).reshape((-1,) + (1,) * (len(extent) - dim - 1))

    loudness = one(*cuts[0])
    for cut in cuts[1:]:
        loudness = loudness * one(*cut)
    return loudness


def gaussian(own_key, shape, deviation, most, cuts=(), kind=jnp.bfloat16):
    factor_of = levels(own_key, shape, cuts, -0.22, 0.18) if cuts else 1.0
    result = jax.random.normal(own_key, shape, jnp.float32) * deviation * factor_of
    return jnp.minimum(jnp.maximum(result, -most), most).astype(kind)


def setup_inputs(seed: int = 0) -> dict:
    splits = jax.random.split(jax.random.key(seed), 8)
    return {
        "tokens": gaussian(splits[0], (TOKENS, D), 1.0, 6.0, ((0, 4), (1, 8))),
        "grad_out": gaussian(splits[1], (TOKENS, D), 0.25, 1.5, ((0, 4), (1, 8))),
        "routes": draw_routes(jax.random.fold_in(splits[7], 71), 0),
        "route_weights": jnp.clip(jnp.exp(math.log(1.0) - 2.3025851 * jax.random.uniform(splits[3], (TOKENS, TOP), jnp.float32) ** levels(splits[3], (TOKENS, TOP), ((0, 4),), -0.2, 0.2)), 0.1, 1.0),
        "gate_weight": gaussian(splits[4], (N_GRP, HALF, D), D ** -0.5, 0.09375, ((0, 4),)),
        "up_weight": gaussian(splits[5], (N_GRP, HALF, D), D ** -0.5, 0.09375, ((0, 4),)),
        "down_weight": gaussian(splits[6], (N_GRP, HALF, D), FF ** -0.5, 0.21875, ((0, 4),)),
    }


def half_terms(rows_in, rows_back, gate_half, up_half, down_half):
    contract = (((1,), (1,)), ((), ()))
    gate_pre = lax.dot_general(rows_in, gate_half, contract, preferred_element_type=jnp.float32)
    up_pre = lax.dot_general(rows_in, up_half, contract, preferred_element_type=jnp.float32)
    back_proj = lax.dot_general(rows_back, down_half, contract, preferred_element_type=jnp.float32)
    sigmoid_gate = jax.nn.sigmoid(gate_pre)
    active = gate_pre * sigmoid_gate
    hidden = (active * up_pre).astype(jnp.bfloat16)
    hidden = lax.optimization_barrier(hidden)
    inner_sum = jnp.sum(hidden.astype(jnp.float32) * back_proj, axis=1)
    grad_gate_pre = (back_proj * up_pre * sigmoid_gate * (1.0 + gate_pre * (1.0 - sigmoid_gate))).astype(jnp.bfloat16)
    grad_up_pre = (back_proj * active).astype(jnp.bfloat16)
    partial_value = jnp.dot(grad_gate_pre, gate_half, preferred_element_type=jnp.float32)
    partial_value = partial_value + jnp.dot(grad_up_pre, up_half, preferred_element_type=jnp.float32)
    return inner_sum, partial_value.astype(jnp.bfloat16)


def reference(tokens, grad_out, routes, route_weights, gate_weight, up_weight, down_weight):
    flat_expert = routes.reshape(-1).astype(jnp.int32)
    flat_token = (jnp.arange(TOKENS * TOP, dtype=jnp.int32) // TOP).astype(jnp.int32)
    flat_weight = route_weights.reshape(-1)
    row_limit = N_GRP * CAP

    def per_expert(state_pair, expert):
        grad_acc, gate_acc = state_pair
        chosen = jnp.argsort((flat_expert != expert).astype(jnp.int32), stable=True)[:row_limit].astype(jnp.int32)
        matched = flat_expert[chosen] == expert
        token_index = flat_token[chosen]
        rows_in = tokens[token_index]
        rows_back = grad_out[token_index]
        inner_first, part_first = half_terms(rows_in, rows_back, gate_weight[expert], up_weight[expert], down_weight[expert])
        other_half = expert + EXPERTS
        inner_second, part_second = half_terms(rows_in, rows_back, gate_weight[other_half], up_weight[other_half], down_weight[other_half])
        pair_sum = (part_first.astype(grad_acc.dtype) + part_second.astype(grad_acc.dtype)).astype(jnp.bfloat16)
        pair_sum = lax.optimization_barrier(pair_sum)
        route_scale = jnp.where(matched, flat_weight[chosen], jnp.zeros_like(flat_weight[chosen]))
        contrib = route_scale[:, None] * pair_sum.astype(grad_acc.dtype)
        grad_acc = grad_acc.at[token_index].add(contrib)
        gate_acc = gate_acc.at[chosen].add(jnp.where(matched, inner_first + inner_second, jnp.zeros_like(inner_first)))
        return (grad_acc, gate_acc), None

    start = (jnp.zeros((TOKENS, D), jnp.float32), jnp.zeros((TOKENS * TOP,), jnp.float32))
    (grad_acc, gate_acc), unused = lax.scan(per_expert, start, jnp.arange(EXPERTS, dtype=jnp.int32))
    return grad_acc.astype(jnp.bfloat16), gate_acc.reshape(TOKENS, TOP)
```

```python
import jax
import jax.numpy as jnp
from jax import lax
from jax.sharding import PartitionSpec as P

TOP = 2
EXTRA = 128


def half_terms(rows_in, rows_back, gate_half, up_half, down_half):
    contract = (((1,), (1,)), ((), ()))
    gate_pre = lax.dot_general(rows_in, gate_half, contract, preferred_element_type=jnp.float32)
    up_pre = lax.dot_general(rows_in, up_half, contract, preferred_element_type=jnp.float32)
    back_proj = lax.dot_general(rows_back, down_half, contract, preferred_element_type=jnp.float32)
    sigmoid_gate = jax.nn.sigmoid(gate_pre)
    active = gate_pre * sigmoid_gate
    hidden = (active * up_pre).astype(jnp.bfloat16)
    hidden = lax.optimization_barrier(hidden)
    inner_sum = jnp.sum(hidden.astype(jnp.float32) * back_proj, axis=1)
    grad_gate_pre = (
        back_proj * up_pre * sigmoid_gate * (1.0 + gate_pre * (1.0 - sigmoid_gate))
    ).astype(jnp.bfloat16)
    grad_up_pre = (back_proj * active).astype(jnp.bfloat16)
    partial_value = jnp.dot(grad_gate_pre, gate_half, preferred_element_type=jnp.float32)
    partial_value = partial_value + jnp.dot(
        grad_up_pre, up_half, preferred_element_type=jnp.float32
    )
    return (inner_sum, partial_value.astype(jnp.bfloat16))


def split_float(value):
    first = value.astype(jnp.bfloat16)
    rest = value - first.astype(jnp.float32)
    second = rest.astype(jnp.bfloat16)
    third = (rest - second.astype(jnp.float32)).astype(jnp.bfloat16)
    return jnp.stack([first, second, third], axis=-1)


def slot_tables(routes, pair_count, rank_count, cap):
    flat_expert = routes.reshape(-1)
    route_total = flat_expert.shape[0]
    onehot = (flat_expert[:, None] == jnp.arange(pair_count, dtype=jnp.int32)[None, :]).astype(
        jnp.int32
    )
    running = jnp.cumsum(onehot, axis=0)
    slot_index = flat_expert * cap + jnp.sum((running - 1) * onehot, axis=1)
    slot_total = pair_count * cap
    source_token = (
        jnp.zeros((slot_total,), jnp.int32)
        .at[slot_index]
        .set(jnp.arange(route_total, dtype=jnp.int32) // TOP)
    )
    filled = jnp.zeros((slot_total,), jnp.bool_).at[slot_index].set(True)
    return slot_index, source_token, filled


def on_device(tokens, grad_out, routes, route_weights, gate_weight, up_weight, down_weight):
    group_count = lax.axis_size("grp")
    rank_count = lax.axis_size("ep")
    pair_count = group_count // 2
    both = ("grp", "ep")
    group_tokens, feat_width = tokens.shape
    full_width = feat_width * rank_count
    per_device = group_tokens // rank_count
    slots = 2 * ((per_device * TOP + 2 * pair_count - 1) // (2 * pair_count))
    cap = rank_count * slots
    dense = pair_count == TOP and cap == group_tokens

    def by_half(values):
        blocks = values.reshape(-1, pair_count, rank_count, slots, values.shape[-1])
        return jnp.broadcast_to(blocks, (2,) + blocks.shape[1:])

    paired = jnp.concatenate([tokens, grad_out], axis=1)
    if dense:
        packed = jnp.broadcast_to(paired[None], (pair_count,) + paired.shape)
    else:
        slot_index, source_token, filled = slot_tables(routes, pair_count, rank_count, cap)
        packed = jnp.where(filled[:, None], paired[source_token], jnp.zeros((), paired.dtype))
    send = by_half(packed).reshape(group_count * rank_count, slots, 2 * feat_width)
    held = lax.all_to_all(send, both, split_axis=0, concat_axis=0, tiled=True)
    held = held.reshape(group_count, rank_count, slots, 2, feat_width)
    held = held.transpose(3, 0, 2, 1, 4).reshape(2, group_count * slots, full_width)
    inner_sum, partial_value = half_terms(
        held[0], held[1], gate_weight[0], up_weight[0], down_weight[0]
    )
    back = partial_value.reshape(group_count, slots, rank_count, feat_width).transpose(0, 2, 1, 3)
    parts = split_float(inner_sum).reshape(group_count, 1, slots, 3)
    parts = jnp.pad(parts, ((0, 0), (0, 0), (0, 0), (0, EXTRA - 3)))
    parts = jnp.broadcast_to(parts, (group_count, rank_count, slots, EXTRA))
    back = jnp.concatenate([back, parts], axis=-1)
    back = back.reshape(group_count * rank_count, slots, feat_width + EXTRA)
    arrived = lax.all_to_all(back, both, split_axis=0, concat_axis=0, tiled=True)
    arrived = arrived.reshape(2, pair_count, cap, feat_width + EXTRA)
    value = arrived[..., :feat_width].astype(jnp.float32)
    inner = jnp.sum(arrived[..., feat_width : feat_width + 3].astype(jnp.float32), axis=(0, 3))
    pair_sum = value[0] + value[1]
    if dense:
        first_expert = routes[:, :1] == 0
        weight_first = jnp.where(first_expert, route_weights[:, :1], route_weights[:, 1:])
        weight_second = jnp.where(first_expert, route_weights[:, 1:], route_weights[:, :1])
        grad_tokens = pair_sum[0] * weight_first + pair_sum[1] * weight_second
        grad_gates = jnp.where(routes == 0, inner[0][:, None], inner[1][:, None])
    else:
        per_route = pair_sum.reshape(pair_count * cap, feat_width)[slot_index]
        weighted = per_route.reshape(group_tokens, TOP, feat_width) * route_weights[:, :, None]
        grad_tokens = jnp.sum(weighted, axis=1)
        grad_gates = inner.reshape(-1)[slot_index].reshape(group_tokens, TOP)
    return (grad_tokens.astype(jnp.bfloat16), grad_gates)


def solution(mesh):
    placed = (
        P("grp", "ep"),
        P("grp", "ep"),
        P("grp", None),
        P("grp", None),
        P("grp", None, None),
        P("grp", None, None),
        P("grp", None, None),
    )
    return jax.shard_map(
        on_device,
        mesh=mesh,
        in_specs=placed,
        out_specs=(P("grp", "ep"), P("grp", None)),
        check_vma=False,
    )
```

```python
import jax
import jax.numpy as jnp
from jax import lax
from jax.experimental import pallas as pl
from jax.experimental.pallas import tpu as pltpu
from jax.sharding import PartitionSpec as P

TOP = 2
LANES = 128
PARTS = 3
VMEM_BYTES = 40 * 1024 * 1024


def gradients(gate_pre, up_pre, back_proj):
    sigmoid_gate = jax.nn.sigmoid(gate_pre)
    active = gate_pre * sigmoid_gate
    hidden = (active * up_pre).astype(jnp.bfloat16)
    product = hidden.astype(jnp.float32) * back_proj
    grad_gate_pre = back_proj * up_pre * sigmoid_gate * (1.0 + gate_pre * (1.0 - sigmoid_gate))
    grad_up_pre = back_proj * active
    return product, grad_gate_pre.astype(jnp.bfloat16), grad_up_pre.astype(jnp.bfloat16)


def times_rows(rows, weight):
    contract = (((1,), (1,)), ((), ()))
    return lax.dot_general(rows, weight, contract, preferred_element_type=jnp.float32)


def times_units(grads, weight):
    return jnp.dot(grads, weight, preferred_element_type=jnp.float32)


def split_float(value):
    first = value.astype(jnp.bfloat16).astype(jnp.float32)
    second = (value - first).astype(jnp.bfloat16).astype(jnp.float32)
    third = (value - first - second).astype(jnp.bfloat16).astype(jnp.float32)
    return first, second, third


def repeat_lanes(row, start, count):
    lane = lax.broadcasted_iota(jnp.int32, row.shape, 1)
    row = jnp.where((lane >= start) & (lane < start + count), row, 0.0)
    row = pltpu.roll(row, (LANES - start) % LANES, 1)
    while count < LANES:
        row = row + pltpu.roll(row, count, 1)
        count *= 2
    return row


def half_kernel(rows_ref, gate_ref, up_hbm, down_hbm, out_ref, up_ref, down_ref, arrived):
    group_count, rank_count, slots, width = rows_ref.shape
    width = width // 2
    total = group_count * slots
    copies = (
        pltpu.make_async_copy(up_hbm, up_ref, arrived.at[0]),
        pltpu.make_async_copy(down_hbm, down_ref, arrived.at[1]),
    )
    for copy in copies:
        copy.start()
    slices = [slice(rank * width, (rank + 1) * width) for rank in range(rank_count)]

    def project(lanes, weight_ref):
        value = 0.0
        for rank, columns in enumerate(slices):
            rows = rows_ref[:, rank, :, lanes].reshape(total, width)
            value = value + times_rows(rows, weight_ref[0, :, columns])
        return value

    gate_pre = project(slice(0, width), gate_ref)
    copies[0].wait()
    up_pre = project(slice(0, width), up_ref)
    copies[1].wait()
    back_proj = project(slice(width, 2 * width), down_ref)
    product, grad_gate_pre, grad_up_pre = gradients(gate_pre, up_pre, back_proj)

    folded = product[:, :LANES]
    for start in range(LANES, product.shape[1], LANES):
        folded = folded + product[:, start : start + LANES]
    folded = jnp.concatenate([folded, jnp.zeros((LANES - total, LANES), jnp.float32)], axis=0)
    inner_sum = jnp.sum(folded.T, axis=0, keepdims=True)
    extra = out_ref.shape[2] - slots * (width // LANES)
    line = lax.broadcasted_iota(jnp.int32, (extra, LANES), 0)
    for group in range(group_count):
        tail = jnp.zeros((extra, LANES), jnp.float32)
        for index, piece in enumerate(split_float(repeat_lanes(inner_sum, group * slots, slots))):
            tail = jnp.where(line == index, piece, tail)
        for rank in range(rank_count):
            out_ref[group, rank, slots * (width // LANES) :, :] = tail.astype(jnp.bfloat16)

    for rank, columns in enumerate(slices):
        partial = times_units(grad_gate_pre, gate_ref[0, :, columns])
        partial = partial + times_units(grad_up_pre, up_ref[0, :, columns])
        partial = partial.astype(jnp.bfloat16)
        for group in range(group_count):
            rows = slice(group * slots, (group + 1) * slots)
            for index in range(width // LANES):
                lanes = slice(index * LANES, (index + 1) * LANES)
                out_ref[group, rank, index * slots : (index + 1) * slots, :] = partial[rows, lanes]


def owner_kernel(parts_ref, routes_ref, weights_ref, grad_ref, gates_ref):
    _, rank_count, length, _ = parts_ref.shape
    total, width = grad_ref.shape
    slots = total // rank_count
    body = slots * (width // LANES)
    first = routes_ref[:1, :] == 0
    scale_first = jnp.where(first, weights_ref[:1, :], weights_ref[1:, :])
    scale_second = jnp.where(first, weights_ref[1:, :], weights_ref[:1, :])
    line = lax.broadcasted_iota(jnp.int32, (LANES, total), 0)
    turned = jnp.where(line == 0, scale_first, scale_second).T
    scales = (turned[:, :1], turned[:, 1:2])
    for rank in range(rank_count):
        rows = slice(rank * slots, (rank + 1) * slots)
        for index in range(width // LANES):
            place = slice(index * slots, (index + 1) * slots)
            value = 0.0
            for expert in range(TOP):
                pair = parts_ref[expert, rank, place, :].astype(jnp.float32)
                pair = pair + parts_ref[expert + TOP, rank, place, :].astype(jnp.float32)
                value = value + scales[expert][rows] * pair
            grad_ref[rows, index * LANES : (index + 1) * LANES] = value.astype(jnp.bfloat16)
    owner = lax.broadcasted_iota(jnp.int32, (length - body, LANES), 1) // slots
    inner = []
    for expert in range(TOP):
        value = jnp.zeros((length - body, LANES), jnp.float32)
        for rank in range(rank_count):
            pair = parts_ref[expert, rank, body:, :].astype(jnp.float32)
            pair = pair + parts_ref[expert + TOP, rank, body:, :].astype(jnp.float32)
            value = value + jnp.where(owner == rank, pair, 0.0)
        inner.append(jnp.sum(value, axis=0, keepdims=True))
    gates_ref[...] = jnp.where(routes_ref[...] == 0, inner[0], inner[1])


def every_expert(tokens, grad_out, routes, route_weights, gate_weight, up_weight, down_weight):
    group_count = lax.axis_size("grp")
    rank_count = lax.axis_size("ep")
    both = ("grp", "ep")
    group_tokens, width = tokens.shape
    slots = group_tokens // rank_count
    length = slots * (width // LANES) + 8
    whole = pl.BlockSpec(memory_space=pltpu.VMEM)
    there = pl.BlockSpec(memory_space=pltpu.HBM)
    params = pltpu.CompilerParams(vmem_limit_bytes=VMEM_BYTES)

    paired = jnp.concatenate([tokens, grad_out], axis=1)
    send = jnp.broadcast_to(paired[None], (group_count,) + paired.shape)
    send = send.reshape(group_count * rank_count, slots, 2 * width)
    held = lax.all_to_all(send, both, split_axis=0, concat_axis=0, tiled=True)
    back = pl.pallas_call(
        half_kernel,
        out_shape=jax.ShapeDtypeStruct((group_count, rank_count, length, LANES), jnp.bfloat16),
        in_specs=[whole, whole, there, there],
        out_specs=whole,
        scratch_shapes=[
            pltpu.VMEM(up_weight.shape, up_weight.dtype),
            pltpu.VMEM(down_weight.shape, down_weight.dtype),
            pltpu.SemaphoreType.DMA((2,)),
        ],
        compiler_params=params,
    )(
        held.reshape(group_count, rank_count, slots, 2 * width),
        gate_weight,
        up_weight,
        down_weight,
    )
    back = back.reshape(group_count * rank_count, length, LANES)
    arrived = lax.all_to_all(back, both, split_axis=0, concat_axis=0, tiled=True)
    grad_tokens, grad_gates = pl.pallas_call(
        owner_kernel,
        out_shape=(
            jax.ShapeDtypeStruct(tokens.shape, jnp.bfloat16),
            jax.ShapeDtypeStruct((TOP, group_tokens), jnp.float32),
        ),
        in_specs=[whole] * 3,
        out_specs=(whole, whole),
        compiler_params=params,
    )(arrived.reshape(group_count, rank_count, length, LANES), routes.T, route_weights.T)
    return grad_tokens, grad_gates.T


def slot_tables(routes, pair_count, cap):
    flat_expert = routes.reshape(-1)
    route_total = flat_expert.shape[0]
    onehot = (flat_expert[:, None] == jnp.arange(pair_count, dtype=jnp.int32)[None, :]).astype(
        jnp.int32
    )
    running = jnp.cumsum(onehot, axis=0)
    slot_index = flat_expert * cap + jnp.sum((running - 1) * onehot, axis=1)
    slot_total = pair_count * cap
    source_token = (
        jnp.zeros((slot_total,), jnp.int32)
        .at[slot_index]
        .set(jnp.arange(route_total, dtype=jnp.int32) // TOP)
    )
    filled = jnp.zeros((slot_total,), jnp.bool_).at[slot_index].set(True)
    return slot_index, source_token, filled


def by_slots(tokens, grad_out, routes, route_weights, gate_weight, up_weight, down_weight):
    group_count = lax.axis_size("grp")
    rank_count = lax.axis_size("ep")
    pair_count = group_count // 2
    both = ("grp", "ep")
    group_tokens, width = tokens.shape
    per_device = group_tokens // rank_count
    slots = 2 * ((per_device * TOP + 2 * pair_count - 1) // (2 * pair_count))
    cap = rank_count * slots
    extra = LANES
    slot_index, source_token, filled = slot_tables(routes, pair_count, cap)

    paired = jnp.concatenate([tokens, grad_out], axis=1)
    packed = jnp.where(filled[:, None], paired[source_token], jnp.zeros((), paired.dtype))
    send = packed.reshape(1, pair_count, rank_count, slots, 2 * width)
    send = jnp.broadcast_to(send, (2,) + send.shape[1:])
    send = send.reshape(group_count * rank_count, slots, 2 * width)
    held = lax.all_to_all(send, both, split_axis=0, concat_axis=0, tiled=True)
    held = held.reshape(group_count, rank_count, slots, 2, width)
    held = held.transpose(3, 0, 2, 1, 4).reshape(2, group_count * slots, rank_count * width)
    gate_pre = times_rows(held[0], gate_weight[0])
    up_pre = times_rows(held[0], up_weight[0])
    back_proj = times_rows(held[1], down_weight[0])
    product, grad_gate_pre, grad_up_pre = gradients(gate_pre, up_pre, back_proj)
    inner_sum = jnp.sum(product, axis=1, keepdims=True)
    partial = times_units(grad_gate_pre, gate_weight[0]) + times_units(grad_up_pre, up_weight[0])
    back = partial.astype(jnp.bfloat16).reshape(group_count, slots, rank_count, width)
    back = back.transpose(0, 2, 1, 3)
    parts = jnp.concatenate(split_float(inner_sum), axis=1).astype(jnp.bfloat16)
    parts = jnp.pad(parts, ((0, 0), (0, extra - PARTS))).reshape(group_count, 1, slots, extra)
    parts = jnp.broadcast_to(parts, (group_count, rank_count, slots, extra))
    back = jnp.concatenate([back, parts], axis=-1)
    back = back.reshape(group_count * rank_count, slots, width + extra)
    arrived = lax.all_to_all(back, both, split_axis=0, concat_axis=0, tiled=True)
    arrived = arrived.reshape(2, pair_count * cap, width + extra).astype(jnp.float32)
    per_route = (arrived[0] + arrived[1])[slot_index].reshape(group_tokens, TOP, width + extra)
    grad_tokens = jnp.sum(per_route[..., :width] * route_weights[:, :, None], axis=1)
    grad_gates = jnp.sum(per_route[..., width : width + PARTS], axis=2)
    return (grad_tokens.astype(jnp.bfloat16), grad_gates)


def on_device(*args):
    pair_count = lax.axis_size("grp") // 2
    return every_expert(*args) if pair_count == TOP else by_slots(*args)


def solution(mesh):
    placed = (
        P("grp", "ep"),
        P("grp", "ep"),
        P("grp", None),
        P("grp", None),
        P("grp", None, None),
        P("grp", None, None),
        P("grp", None, None),
    )
    return jax.shard_map(
        on_device,
        mesh=mesh,
        in_specs=placed,
        out_specs=(P("grp", "ep"), P("grp", None)),
        check_vma=False,
    )
```

```python
import jax
import jax.numpy as jnp
from jax import lax
from jax.experimental import pallas as pl
from jax.experimental.pallas import tpu as pltpu
from jax.sharding import PartitionSpec as P

TOP = 2
LANES = 128
PARTS = 2
VMEM_BYTES = 40 * 1024 * 1024


def gradients(gate_pre, up_pre, back_proj):
    sigmoid_gate = jax.nn.sigmoid(gate_pre)
    active = gate_pre * sigmoid_gate
    hidden = (active * up_pre).astype(jnp.bfloat16)
    product = hidden.astype(jnp.float32) * back_proj
    grad_gate_pre = back_proj * up_pre * sigmoid_gate * (1.0 + gate_pre * (1.0 - sigmoid_gate))
    grad_up_pre = back_proj * active
    return product, grad_gate_pre.astype(jnp.bfloat16), grad_up_pre.astype(jnp.bfloat16)


def times_rows(rows, weight):
    contract = (((1,), (1,)), ((), ()))
    return lax.dot_general(rows, weight, contract, preferred_element_type=jnp.float32)


def times_units(grads, weight):
    return jnp.dot(grads, weight, preferred_element_type=jnp.float32)


def split_float(value):
    first = value.astype(jnp.bfloat16).astype(jnp.float32)
    second = (value - first).astype(jnp.bfloat16).astype(jnp.float32)
    return first, second


def repeat_lanes(row, start, count):
    lane = lax.broadcasted_iota(jnp.int32, row.shape, 1)
    row = jnp.where((lane >= start) & (lane < start + count), row, 0.0)
    row = pltpu.roll(row, (LANES - start) % LANES, 1)
    while count < LANES:
        row = row + pltpu.roll(row, count, 1)
        count *= 2
    return row


def pack_kernel(tokens_hbm, grad_hbm, up_hbm, out_ref, up_ref, tokens_ref, grad_ref, arrived):
    width = tokens_ref.shape[1]
    copies = [
        pltpu.make_async_copy(tokens_hbm, tokens_ref, arrived.at[0]),
        pltpu.make_async_copy(grad_hbm, grad_ref, arrived.at[1]),
        pltpu.make_async_copy(up_hbm, up_ref, arrived.at[2]),
    ]
    for copy in copies:
        copy.start()
    copies[0].wait()
    for group in range(out_ref.shape[0]):
        out_ref[group, :, :width] = tokens_ref[...]
    copies[1].wait()
    for group in range(out_ref.shape[0]):
        out_ref[group, :, width:] = grad_ref[...]
    copies[2].wait()


def half_kernel(rows_ref, gate_ref, up_ref, down_hbm, out_ref, down_ref, arrived):
    group_count, rank_count, slots, width = rows_ref.shape
    width = width // 2
    total = group_count * slots
    slices = [slice(rank * width, (rank + 1) * width) for rank in range(rank_count)]
    copy = pltpu.make_async_copy(down_hbm, down_ref, arrived.at[0])
    copy.start()

    def project(lanes, weight_ref):
        rows = [rows_ref[:, rank, :, lanes].reshape(total, width) for rank in range(rank_count)]
        return times_rows(jnp.concatenate(rows, axis=1), weight_ref[0])

    first, second = slice(0, width), slice(width, 2 * width)
    gate_pre = project(first, gate_ref)
    up_pre = project(first, up_ref)
    copy.wait()
    back_proj = project(second, down_ref)
    product, by_gate, by_up = gradients(gate_pre, up_pre, back_proj)

    folded = product[:, :LANES]
    for start in range(LANES, product.shape[1], LANES):
        folded = folded + product[:, start : start + LANES]
    folded = jnp.concatenate([folded, jnp.zeros((LANES - total, LANES), jnp.float32)], axis=0)
    inner_sum = jnp.sum(folded.T, axis=0, keepdims=True)
    line = lax.broadcasted_iota(jnp.int32, (2, LANES), 0)
    for group in range(group_count):
        tail = jnp.zeros((2, LANES), jnp.float32)
        for index, piece in enumerate(split_float(repeat_lanes(inner_sum, group * slots, slots))):
            tail = jnp.where(line == index, piece, tail)
        for rank in range(rank_count):
            out_ref[group, rank, slots * (width // LANES) // 2] = tail.astype(jnp.bfloat16)

    for rank, columns in enumerate(slices):
        partial = times_units(by_gate, gate_ref[0, :, columns])
        partial = partial + times_units(by_up, up_ref[0, :, columns])
        partial = partial.astype(jnp.bfloat16)
        for group in range(group_count):
            rows = slice(group * slots, (group + 1) * slots)
            for index in range(width // LANES):
                lanes = slice(index * LANES, (index + 1) * LANES)
                place = slice(index * slots // 2, (index + 1) * slots // 2)
                out_ref[group, rank, place] = partial[rows, lanes].reshape(slots // 2, 2, LANES)


def owner_kernel(parts_ref, routes_ref, weights_ref, grad_ref, gates_ref):
    _, rank_count, length, _, _ = parts_ref.shape
    total, width = grad_ref.shape
    slots = total // rank_count
    body = slots * (width // LANES) // 2
    first = routes_ref[:1, :] == 0
    scale_first = jnp.where(first, weights_ref[:1, :], weights_ref[1:, :])
    scale_second = jnp.where(first, weights_ref[1:, :], weights_ref[:1, :])
    line = lax.broadcasted_iota(jnp.int32, (LANES, total), 0)
    turned = jnp.where(line == 0, scale_first, scale_second).T
    scales = (turned[:, :1], turned[:, 1:2])
    for rank in range(rank_count):
        rows = slice(rank * slots, (rank + 1) * slots)
        for index in range(width // LANES):
            place = slice(index * slots // 2, (index + 1) * slots // 2)
            value = 0.0
            for expert in range(TOP):
                pair = parts_ref[expert, rank, place].reshape(slots, LANES).astype(jnp.float32)
                pair = pair + parts_ref[expert + TOP, rank, place].reshape(slots, LANES).astype(jnp.float32)
                value = value + scales[expert][rows] * pair
            grad_ref[rows, index * LANES : (index + 1) * LANES] = value.astype(jnp.bfloat16)
    owner = lax.broadcasted_iota(jnp.int32, (2, LANES), 1) // slots
    inner = []
    for expert in range(TOP):
        value = jnp.zeros((2, LANES), jnp.float32)
        for rank in range(rank_count):
            pair = parts_ref[expert, rank, body].astype(jnp.float32)
            pair = pair + parts_ref[expert + TOP, rank, body].astype(jnp.float32)
            value = value + jnp.where(owner == rank, pair, 0.0)
        inner.append(jnp.sum(value, axis=0, keepdims=True))
    gates_ref[...] = jnp.where(routes_ref[...] == 0, inner[0], inner[1])


def every_expert(tokens, grad_out, routes, route_weights, gate_weight, up_weight, down_weight):
    group_count = lax.axis_size("grp")
    rank_count = lax.axis_size("ep")
    both = ("grp", "ep")
    group_tokens, width = tokens.shape
    slots = group_tokens // rank_count
    length = slots * (width // LANES) // 2 + 1
    whole = pl.BlockSpec(memory_space=pltpu.VMEM)
    there = pl.BlockSpec(memory_space=pltpu.HBM)
    params = pltpu.CompilerParams(vmem_limit_bytes=VMEM_BYTES)

    send, up_weight = pl.pallas_call(
        pack_kernel,
        out_shape=[
            jax.ShapeDtypeStruct((group_count, group_tokens, 2 * width), tokens.dtype),
            jax.ShapeDtypeStruct(up_weight.shape, up_weight.dtype),
        ],
        in_specs=[there] * 3,
        out_specs=[whole] * 2,
        scratch_shapes=[
            pltpu.VMEM(tokens.shape, tokens.dtype),
            pltpu.VMEM(tokens.shape, tokens.dtype),
            pltpu.SemaphoreType.DMA((3,)),
        ],
        compiler_params=params,
    )(*[pltpu.with_memory_space_constraint(x, pltpu.HBM) for x in (tokens, grad_out, up_weight)])
    send = send.reshape(group_count * rank_count, slots, 2 * width)
    held = lax.all_to_all(send, both, split_axis=0, concat_axis=0, tiled=True)
    back = pl.pallas_call(
        half_kernel,
        out_shape=jax.ShapeDtypeStruct((group_count, rank_count, length, 2, LANES), jnp.bfloat16),
        in_specs=[whole, whole, whole, there],
        out_specs=whole,
        scratch_shapes=[
            pltpu.VMEM(down_weight.shape, down_weight.dtype),
            pltpu.SemaphoreType.DMA((1,)),
        ],
        compiler_params=params,
    )(
        held.reshape(group_count, rank_count, slots, 2 * width),
        gate_weight,
        up_weight,
        pltpu.with_memory_space_constraint(down_weight, pltpu.HBM),
    )
    back = back.reshape(group_count * rank_count, length, 2, LANES)
    arrived = lax.all_to_all(back, both, split_axis=0, concat_axis=0, tiled=True)
    grad_tokens, grad_gates = pl.pallas_call(
        owner_kernel,
        out_shape=(
            jax.ShapeDtypeStruct(tokens.shape, jnp.bfloat16),
            jax.ShapeDtypeStruct((TOP, group_tokens), jnp.float32),
        ),
        in_specs=[whole] * 3,
        out_specs=(whole, whole),
        compiler_params=params,
    )(arrived.reshape(group_count, rank_count, length, 2, LANES), routes.T, route_weights.T)
    return grad_tokens, grad_gates.T


def slot_tables(routes, pair_count, cap):
    flat_expert = routes.reshape(-1)
    route_total = flat_expert.shape[0]
    onehot = (flat_expert[:, None] == jnp.arange(pair_count, dtype=jnp.int32)[None, :]).astype(
        jnp.int32
    )
    running = jnp.cumsum(onehot, axis=0)
    slot_index = flat_expert * cap + jnp.sum((running - 1) * onehot, axis=1)
    slot_total = pair_count * cap
    source_token = (
        jnp.zeros((slot_total,), jnp.int32)
        .at[slot_index]
        .set(jnp.arange(route_total, dtype=jnp.int32) // TOP)
    )
    filled = jnp.zeros((slot_total,), jnp.bool_).at[slot_index].set(True)
    return slot_index, source_token, filled


def by_slots(tokens, grad_out, routes, route_weights, gate_weight, up_weight, down_weight):
    group_count = lax.axis_size("grp")
    rank_count = lax.axis_size("ep")
    pair_count = group_count // 2
    both = ("grp", "ep")
    group_tokens, width = tokens.shape
    per_device = group_tokens // rank_count
    slots = 2 * ((per_device * TOP + 2 * pair_count - 1) // (2 * pair_count))
    cap = rank_count * slots
    extra = LANES
    slot_index, source_token, filled = slot_tables(routes, pair_count, cap)

    paired = jnp.concatenate([tokens, grad_out], axis=1)
    packed = jnp.where(filled[:, None], paired[source_token], jnp.zeros((), paired.dtype))
    send = packed.reshape(1, pair_count, rank_count, slots, 2 * width)
    send = jnp.broadcast_to(send, (2,) + send.shape[1:])
    send = send.reshape(group_count * rank_count, slots, 2 * width)
    held = lax.all_to_all(send, both, split_axis=0, concat_axis=0, tiled=True)
    held = held.reshape(group_count, rank_count, slots, 2, width)
    held = held.transpose(3, 0, 2, 1, 4).reshape(2, group_count * slots, rank_count * width)
    gate_pre = times_rows(held[0], gate_weight[0])
    up_pre = times_rows(held[0], up_weight[0])
    back_proj = times_rows(held[1], down_weight[0])
    product, grad_gate_pre, grad_up_pre = gradients(gate_pre, up_pre, back_proj)
    inner_sum = jnp.sum(product, axis=1, keepdims=True)
    partial = times_units(grad_gate_pre, gate_weight[0]) + times_units(grad_up_pre, up_weight[0])
    back = partial.astype(jnp.bfloat16).reshape(group_count, slots, rank_count, width)
    back = back.transpose(0, 2, 1, 3)
    parts = jnp.concatenate(split_float(inner_sum), axis=1).astype(jnp.bfloat16)
    parts = jnp.pad(parts, ((0, 0), (0, extra - PARTS))).reshape(group_count, 1, slots, extra)
    parts = jnp.broadcast_to(parts, (group_count, rank_count, slots, extra))
    back = jnp.concatenate([back, parts], axis=-1)
    back = back.reshape(group_count * rank_count, slots, width + extra)
    arrived = lax.all_to_all(back, both, split_axis=0, concat_axis=0, tiled=True)
    arrived = arrived.reshape(2, pair_count * cap, width + extra).astype(jnp.float32)
    per_route = (arrived[0] + arrived[1])[slot_index].reshape(group_tokens, TOP, width + extra)
    grad_tokens = jnp.sum(per_route[..., :width] * route_weights[:, :, None], axis=1)
    grad_gates = jnp.sum(per_route[..., width : width + PARTS], axis=2)
    return (grad_tokens.astype(jnp.bfloat16), grad_gates)


def on_device(*args):
    everywhere = lax.axis_size("grp") // 2 == TOP and args[0].shape[0] == LANES
    return every_expert(*args) if everywhere else by_slots(*args)


def solution(mesh):
    placed = (
        P("grp", "ep"),
        P("grp", "ep"),
        P("grp", None),
        P("grp", None),
        P("grp", None, None),
        P("grp", None, None),
        P("grp", None, None),
    )
    return jax.shard_map(
        on_device,
        mesh=mesh,
        in_specs=placed,
        out_specs=(P("grp", "ep"), P("grp", None)),
        check_vma=False,
    )
```

```python
import jax
import jax.numpy as jnp
from jax import lax
from jax.experimental import pallas as pl
from jax.experimental.pallas import tpu as pltpu
from jax.sharding import PartitionSpec as P

TOP = 2
LANES = 128
PARTS = 2
TILE = 256
VMEM_BYTES = 40 * 1024 * 1024


def gradients(gate_pre, up_pre, back_proj):
    sigmoid_gate = jax.nn.sigmoid(gate_pre)
    active = gate_pre * sigmoid_gate
    hidden = (active * up_pre).astype(jnp.bfloat16)
    product = hidden.astype(jnp.float32) * back_proj
    grad_gate_pre = back_proj * up_pre * sigmoid_gate * (1.0 + gate_pre * (1.0 - sigmoid_gate))
    grad_up_pre = back_proj * active
    return product, grad_gate_pre.astype(jnp.bfloat16), grad_up_pre.astype(jnp.bfloat16)


def times_rows(rows, weight):
    contract = (((1,), (1,)), ((), ()))
    return lax.dot_general(rows, weight, contract, preferred_element_type=jnp.float32)


def times_units(grads, weight):
    return jnp.dot(grads, weight, preferred_element_type=jnp.float32)


def split_float(value):
    first = value.astype(jnp.bfloat16).astype(jnp.float32)
    second = (value - first).astype(jnp.bfloat16).astype(jnp.float32)
    return first, second


def repeat_lanes(row, start, count):
    lane = lax.broadcasted_iota(jnp.int32, row.shape, 1)
    row = jnp.where((lane >= start) & (lane < start + count), row, 0.0)
    row = pltpu.roll(row, (LANES - start) % LANES, 1)
    while count < LANES:
        row = row + pltpu.roll(row, count, 1)
        count *= 2
    return row


def half_kernel(rows_ref, gate_ref, up_ref, down_ref, out_ref):
    group_count, rank_count, slots, width = rows_ref.shape
    width = width // 2
    total = group_count * slots
    slices = [slice(rank * width, (rank + 1) * width) for rank in range(rank_count)]

    units = gate_ref.shape[1]
    cut = units // TILE * TILE
    main, rest = slice(0, cut), slice(cut, units)

    def project(lanes, *weights):
        value = 0.0
        for rank, columns in enumerate(slices):
            rows = rows_ref[:, rank, :, lanes].reshape(total, width)
            block = [ref[0, part, columns] for ref, part in weights]
            block = block[0] if len(block) == 1 else jnp.concatenate(block, axis=0)
            value = value + times_rows(rows, block)
        return value

    first, second = slice(0, width), slice(width, 2 * width)
    gate_main = project(first, (gate_ref, main))
    up_main = project(first, (up_ref, main))
    both_rest = project(first, (gate_ref, rest), (up_ref, rest))
    back_main = project(second, (down_ref, main))
    back_rest = project(second, (down_ref, rest))
    product_main, by_gate_main, by_up_main = gradients(gate_main, up_main, back_main)
    product_rest, by_gate_rest, by_up_rest = gradients(
        both_rest[:, : units - cut], both_rest[:, units - cut :], back_rest
    )
    product = jnp.concatenate([product_main, product_rest], axis=1)
    by_rest = jnp.concatenate([by_gate_rest, by_up_rest], axis=1)

    folded = product[:, :LANES]
    for start in range(LANES, product.shape[1], LANES):
        folded = folded + product[:, start : start + LANES]
    folded = jnp.concatenate([folded, jnp.zeros((LANES - total, LANES), jnp.float32)], axis=0)
    inner_sum = jnp.sum(folded.T, axis=0, keepdims=True)
    line = lax.broadcasted_iota(jnp.int32, (2, LANES), 0)
    for group in range(group_count):
        tail = jnp.zeros((2, LANES), jnp.float32)
        for index, piece in enumerate(split_float(repeat_lanes(inner_sum, group * slots, slots))):
            tail = jnp.where(line == index, piece, tail)
        for rank in range(rank_count):
            out_ref[group, rank, slots * (width // LANES) // 2] = tail.astype(jnp.bfloat16)

    flat_ref = out_ref.reshape(group_count, rank_count, 2 * out_ref.shape[2], LANES)
    for rank, columns in enumerate(slices):
        weight_rest = jnp.concatenate([gate_ref[0, rest, columns], up_ref[0, rest, columns]], axis=0)
        partial = times_units(by_gate_main, gate_ref[0, main, columns])
        partial = partial + times_units(by_up_main, up_ref[0, main, columns])
        partial = partial + times_units(by_rest, weight_rest)
        partial = partial.astype(jnp.bfloat16)
        for group in range(group_count):
            rows = slice(group * slots, (group + 1) * slots)
            for index in range(width // LANES):
                lanes = slice(index * LANES, (index + 1) * LANES)
                flat_ref[group, rank, index * slots : (index + 1) * slots, :] = partial[rows, lanes]


def owner_kernel(parts_ref, routes_ref, weights_ref, grad_ref, gates_ref):
    _, rank_count, length, _, _ = parts_ref.shape
    flat_ref = parts_ref.reshape(parts_ref.shape[0], rank_count, 2 * length, LANES)
    total, width = grad_ref.shape
    slots = total // rank_count
    body = slots * (width // LANES) // 2
    first = routes_ref[:1, :] == 0
    scale_first = jnp.where(first, weights_ref[:1, :], weights_ref[1:, :])
    scale_second = jnp.where(first, weights_ref[1:, :], weights_ref[:1, :])
    line = lax.broadcasted_iota(jnp.int32, (LANES, total), 0)
    turned = jnp.where(line == 0, scale_first, scale_second).T
    scales = (turned[:, :1], turned[:, 1:2])
    for rank in range(rank_count):
        rows = slice(rank * slots, (rank + 1) * slots)
        for index in range(width // LANES):
            place = slice(index * slots, (index + 1) * slots)
            value = 0.0
            for expert in range(TOP):
                pair = flat_ref[expert, rank, place].astype(jnp.float32)
                pair = pair + flat_ref[expert + TOP, rank, place].astype(jnp.float32)
                value = value + scales[expert][rows] * pair
            grad_ref[rows, index * LANES : (index + 1) * LANES] = value.astype(jnp.bfloat16)
    owner = lax.broadcasted_iota(jnp.int32, (2, LANES), 1) // slots
    inner = []
    for expert in range(TOP):
        value = jnp.zeros((2, LANES), jnp.float32)
        for rank in range(rank_count):
            pair = parts_ref[expert, rank, body].astype(jnp.float32)
            pair = pair + parts_ref[expert + TOP, rank, body].astype(jnp.float32)
            value = value + jnp.where(owner == rank, pair, 0.0)
        inner.append(jnp.sum(value, axis=0, keepdims=True))
    gates_ref[...] = jnp.where(routes_ref[...] == 0, inner[0], inner[1])


def every_expert(tokens, grad_out, routes, route_weights, gate_weight, up_weight, down_weight):
    group_count = lax.axis_size("grp")
    rank_count = lax.axis_size("ep")
    both = ("grp", "ep")
    group_tokens, width = tokens.shape
    slots = group_tokens // rank_count
    length = slots * (width // LANES) // 2 + 1
    whole = pl.BlockSpec(memory_space=pltpu.VMEM)
    params = pltpu.CompilerParams(vmem_limit_bytes=VMEM_BYTES)

    paired = jnp.concatenate([tokens, grad_out], axis=1)
    send = jnp.broadcast_to(paired[None], (group_count,) + paired.shape)
    swap = [(source, source ^ 1) for source in range(rank_count)]
    up_weight = lax.ppermute(up_weight, "ep", swap)
    down_weight = lax.ppermute(down_weight, "ep", swap)
    send = send.reshape(group_count * rank_count, slots, 2 * width)
    held = lax.all_to_all(send, both, split_axis=0, concat_axis=0, tiled=True)
    back = pl.pallas_call(
        half_kernel,
        out_shape=jax.ShapeDtypeStruct((group_count, rank_count, length, 2, LANES), jnp.bfloat16),
        in_specs=[whole] * 4,
        out_specs=whole,
        compiler_params=params,
    )(
        held.reshape(group_count, rank_count, slots, 2 * width),
        gate_weight,
        up_weight,
        down_weight,
    )
    back = back.reshape(group_count * rank_count, length, 2, LANES)
    arrived = lax.all_to_all(back, both, split_axis=0, concat_axis=0, tiled=True)
    grad_tokens, grad_gates = pl.pallas_call(
        owner_kernel,
        out_shape=(
            jax.ShapeDtypeStruct(tokens.shape, jnp.bfloat16),
            jax.ShapeDtypeStruct((TOP, group_tokens), jnp.float32),
        ),
        in_specs=[whole] * 3,
        out_specs=(whole, whole),
        compiler_params=params,
    )(arrived.reshape(group_count, rank_count, length, 2, LANES), routes.T, route_weights.T)
    return grad_tokens, grad_gates.T


def slot_tables(routes, pair_count, cap):
    flat_expert = routes.reshape(-1)
    route_total = flat_expert.shape[0]
    onehot = (flat_expert[:, None] == jnp.arange(pair_count, dtype=jnp.int32)[None, :]).astype(
        jnp.int32
    )
    running = jnp.cumsum(onehot, axis=0)
    slot_index = flat_expert * cap + jnp.sum((running - 1) * onehot, axis=1)
    slot_total = pair_count * cap
    source_token = (
        jnp.zeros((slot_total,), jnp.int32)
        .at[slot_index]
        .set(jnp.arange(route_total, dtype=jnp.int32) // TOP)
    )
    filled = jnp.zeros((slot_total,), jnp.bool_).at[slot_index].set(True)
    return slot_index, source_token, filled


def by_slots(tokens, grad_out, routes, route_weights, gate_weight, up_weight, down_weight):
    group_count = lax.axis_size("grp")
    rank_count = lax.axis_size("ep")
    pair_count = group_count // 2
    both = ("grp", "ep")
    group_tokens, width = tokens.shape
    per_device = group_tokens // rank_count
    slots = 2 * ((per_device * TOP + 2 * pair_count - 1) // (2 * pair_count))
    cap = rank_count * slots
    extra = LANES
    slot_index, source_token, filled = slot_tables(routes, pair_count, cap)

    paired = jnp.concatenate([tokens, grad_out], axis=1)
    packed = jnp.where(filled[:, None], paired[source_token], jnp.zeros((), paired.dtype))
    send = packed.reshape(1, pair_count, rank_count, slots, 2 * width)
    send = jnp.broadcast_to(send, (2,) + send.shape[1:])
    send = send.reshape(group_count * rank_count, slots, 2 * width)
    held = lax.all_to_all(send, both, split_axis=0, concat_axis=0, tiled=True)
    held = held.reshape(group_count, rank_count, slots, 2, width)
    held = held.transpose(3, 0, 2, 1, 4).reshape(2, group_count * slots, rank_count * width)
    gate_pre = times_rows(held[0], gate_weight[0])
    up_pre = times_rows(held[0], up_weight[0])
    back_proj = times_rows(held[1], down_weight[0])
    product, grad_gate_pre, grad_up_pre = gradients(gate_pre, up_pre, back_proj)
    inner_sum = jnp.sum(product, axis=1, keepdims=True)
    partial = times_units(grad_gate_pre, gate_weight[0]) + times_units(grad_up_pre, up_weight[0])
    back = partial.astype(jnp.bfloat16).reshape(group_count, slots, rank_count, width)
    back = back.transpose(0, 2, 1, 3)
    parts = jnp.concatenate(split_float(inner_sum), axis=1).astype(jnp.bfloat16)
    parts = jnp.pad(parts, ((0, 0), (0, extra - PARTS))).reshape(group_count, 1, slots, extra)
    parts = jnp.broadcast_to(parts, (group_count, rank_count, slots, extra))
    back = jnp.concatenate([back, parts], axis=-1)
    back = back.reshape(group_count * rank_count, slots, width + extra)
    arrived = lax.all_to_all(back, both, split_axis=0, concat_axis=0, tiled=True)
    arrived = arrived.reshape(2, pair_count * cap, width + extra).astype(jnp.float32)
    per_route = (arrived[0] + arrived[1])[slot_index].reshape(group_tokens, TOP, width + extra)
    grad_tokens = jnp.sum(per_route[..., :width] * route_weights[:, :, None], axis=1)
    grad_gates = jnp.sum(per_route[..., width : width + PARTS], axis=2)
    return (grad_tokens.astype(jnp.bfloat16), grad_gates)


def on_device(*args):
    everywhere = lax.axis_size("grp") // 2 == TOP and args[0].shape[0] == LANES
    everywhere = everywhere and lax.axis_size("ep") % 2 == 0
    return every_expert(*args) if everywhere else by_slots(*args)


def solution(mesh):
    placed = (
        P("grp", "ep"),
        P("grp", "ep"),
        P("grp", None),
        P("grp", None),
        P("grp", None, None),
        P("grp", None, None),
        P("grp", None, None),
    )
    return jax.shard_map(
        on_device,
        mesh=mesh,
        in_specs=placed,
        out_specs=(P("grp", "ep"), P("grp", None)),
        check_vma=False,
    )
```

```python
import jax
import jax.numpy as jnp
from jax import lax
from jax.experimental import pallas as pl
from jax.experimental.pallas import tpu as pltpu
from jax.sharding import PartitionSpec as P

TOP = 2
LANES = 128
PARTS = 2
TILE = 256
VMEM_BYTES = 40 * 1024 * 1024


def gradients(gate_pre, up_pre, back_proj):
    sigmoid_gate = jax.nn.sigmoid(gate_pre)
    active = gate_pre * sigmoid_gate
    hidden = (active * up_pre).astype(jnp.bfloat16)
    product = hidden.astype(jnp.float32) * back_proj
    grad_gate_pre = back_proj * up_pre * sigmoid_gate * (1.0 + gate_pre * (1.0 - sigmoid_gate))
    grad_up_pre = back_proj * active
    return product, grad_gate_pre.astype(jnp.bfloat16), grad_up_pre.astype(jnp.bfloat16)


def times_rows(rows, weight):
    contract = (((1,), (1,)), ((), ()))
    return lax.dot_general(rows, weight, contract, preferred_element_type=jnp.float32)


def times_units(grads, weight):
    return jnp.dot(grads, weight, preferred_element_type=jnp.float32)


def split_float(value):
    first = value.astype(jnp.bfloat16).astype(jnp.float32)
    second = (value - first).astype(jnp.bfloat16).astype(jnp.float32)
    return first, second


def repeat_lanes(row, start, count):
    lane = lax.broadcasted_iota(jnp.int32, row.shape, 1)
    row = jnp.where((lane >= start) & (lane < start + count), row, 0.0)
    row = pltpu.roll(row, (LANES - start) % LANES, 1)
    while count < LANES:
        row = row + pltpu.roll(row, count, 1)
        count *= 2
    return row


def half_kernel(rows_ref, gate_ref, up_ref, down_ref, out_ref):
    rank_count, group_count, slots, width = rows_ref.shape
    width = width // 2
    total = group_count * slots
    slices = [slice(rank * width, (rank + 1) * width) for rank in range(rank_count)]

    units = gate_ref.shape[1]
    cut = units // TILE * TILE
    main, rest = slice(0, cut), slice(cut, units)

    def project(lanes, *weights):
        value = 0.0
        for rank, columns in enumerate(slices):
            rows = rows_ref[rank, :, :, lanes].reshape(total, width)
            block = [ref[0, part, columns] for ref, part in weights]
            block = block[0] if len(block) == 1 else jnp.concatenate(block, axis=0)
            value = value + times_rows(rows, block)
        return value

    first, second = slice(0, width), slice(width, 2 * width)
    gate_main = project(first, (gate_ref, main))
    up_main = project(first, (up_ref, main))
    both_rest = project(first, (gate_ref, rest), (up_ref, rest))
    back_main = project(second, (down_ref, main))
    back_rest = project(second, (down_ref, rest))
    product_main, by_gate_main, by_up_main = gradients(gate_main, up_main, back_main)
    product_rest, by_gate_rest, by_up_rest = gradients(
        both_rest[:, : units - cut], both_rest[:, units - cut :], back_rest
    )
    product = jnp.concatenate([product_main, product_rest], axis=1)
    by_rest = jnp.concatenate([by_gate_rest, by_up_rest], axis=1)

    folded = product[:, :LANES]
    for start in range(LANES, product.shape[1], LANES):
        folded = folded + product[:, start : start + LANES]
    folded = jnp.concatenate([folded, jnp.zeros((LANES - total, LANES), jnp.float32)], axis=0)
    inner_sum = jnp.sum(folded.T, axis=0, keepdims=True)
    line = lax.broadcasted_iota(jnp.int32, (2, LANES), 0)
    for group in range(group_count):
        tail = jnp.zeros((2, LANES), jnp.float32)
        for index, piece in enumerate(split_float(repeat_lanes(inner_sum, group * slots, slots))):
            tail = jnp.where(line == index, piece, tail)
        for rank in range(rank_count):
            out_ref[rank, group, slots * (width // LANES) // 2] = tail.astype(jnp.bfloat16)

    flat_ref = out_ref.reshape(rank_count, group_count, 2 * out_ref.shape[2], LANES)
    for rank, columns in enumerate(slices):
        weight_rest = jnp.concatenate([gate_ref[0, rest, columns], up_ref[0, rest, columns]], axis=0)
        partial = times_units(by_gate_main, gate_ref[0, main, columns])
        partial = partial + times_units(by_up_main, up_ref[0, main, columns])
        partial = partial + times_units(by_rest, weight_rest)
        partial = partial.astype(jnp.bfloat16)
        for group in range(group_count):
            rows = slice(group * slots, (group + 1) * slots)
            for index in range(width // LANES):
                lanes = slice(index * LANES, (index + 1) * LANES)
                flat_ref[rank, group, index * slots : (index + 1) * slots, :] = partial[rows, lanes]


def owner_kernel(parts_ref, routes_ref, weights_ref, grad_ref, gates_ref):
    rank_count, _, length, _, _ = parts_ref.shape
    flat_ref = parts_ref.reshape(rank_count, parts_ref.shape[1], 2 * length, LANES)
    total, width = grad_ref.shape
    slots = total // rank_count
    body = slots * (width // LANES) // 2
    first = routes_ref[:1, :] == 0
    scale_first = jnp.where(first, weights_ref[:1, :], weights_ref[1:, :])
    scale_second = jnp.where(first, weights_ref[1:, :], weights_ref[:1, :])
    line = lax.broadcasted_iota(jnp.int32, (LANES, total), 0)
    turned = jnp.where(line == 0, scale_first, scale_second).T
    scales = (turned[:, :1], turned[:, 1:2])
    for rank in range(rank_count):
        rows = slice(rank * slots, (rank + 1) * slots)
        for index in range(width // LANES):
            place = slice(index * slots, (index + 1) * slots)
            value = 0.0
            for expert in range(TOP):
                pair = flat_ref[rank, expert, place].astype(jnp.float32)
                pair = pair + flat_ref[rank, expert + TOP, place].astype(jnp.float32)
                value = value + scales[expert][rows] * pair
            grad_ref[rows, index * LANES : (index + 1) * LANES] = value.astype(jnp.bfloat16)
    owner = lax.broadcasted_iota(jnp.int32, (2, LANES), 1) // slots
    inner = []
    for expert in range(TOP):
        value = jnp.zeros((2, LANES), jnp.float32)
        for rank in range(rank_count):
            pair = parts_ref[rank, expert, body].astype(jnp.float32)
            pair = pair + parts_ref[rank, expert + TOP, body].astype(jnp.float32)
            value = value + jnp.where(owner == rank, pair, 0.0)
        inner.append(jnp.sum(value, axis=0, keepdims=True))
    gates_ref[...] = jnp.where(routes_ref[...] == 0, inner[0], inner[1])


def every_expert(tokens, grad_out, routes, route_weights, gate_weight, up_weight, down_weight):
    group_count = lax.axis_size("grp")
    rank_count = lax.axis_size("ep")
    both = ("ep", "grp")
    group_tokens, width = tokens.shape
    slots = group_tokens // rank_count
    length = slots * (width // LANES) // 2 + 1
    whole = pl.BlockSpec(memory_space=pltpu.VMEM)
    params = pltpu.CompilerParams(vmem_limit_bytes=VMEM_BYTES)

    paired = jnp.concatenate([tokens, grad_out], axis=1).reshape(rank_count, 1, slots, 2 * width)
    send = jnp.broadcast_to(paired, (rank_count, group_count, slots, 2 * width))
    swap = [(source, source ^ 1) for source in range(rank_count)]
    send, up_weight, down_weight = lax.optimization_barrier((send, up_weight, down_weight))
    up_weight = lax.ppermute(up_weight, "ep", swap)
    down_weight = lax.ppermute(down_weight, "ep", swap)
    send = send.reshape(group_count * rank_count, slots, 2 * width)
    held = lax.all_to_all(send, both, split_axis=0, concat_axis=0, tiled=True)
    back = pl.pallas_call(
        half_kernel,
        out_shape=jax.ShapeDtypeStruct((rank_count, group_count, length, 2, LANES), jnp.bfloat16),
        in_specs=[whole] * 4,
        out_specs=whole,
        compiler_params=params,
    )(
        held.reshape(rank_count, group_count, slots, 2 * width),
        gate_weight,
        up_weight,
        down_weight,
    )
    back = back.reshape(group_count * rank_count, length, 2, LANES)
    arrived = lax.all_to_all(back, both, split_axis=0, concat_axis=0, tiled=True)
    grad_tokens, grad_gates = pl.pallas_call(
        owner_kernel,
        out_shape=(
            jax.ShapeDtypeStruct(tokens.shape, jnp.bfloat16),
            jax.ShapeDtypeStruct((TOP, group_tokens), jnp.float32),
        ),
        in_specs=[whole] * 3,
        out_specs=(whole, whole),
        compiler_params=params,
    )(arrived.reshape(rank_count, group_count, length, 2, LANES), routes.T, route_weights.T)
    return grad_tokens, grad_gates.T


def slot_tables(routes, pair_count, cap):
    flat_expert = routes.reshape(-1)
    route_total = flat_expert.shape[0]
    onehot = (flat_expert[:, None] == jnp.arange(pair_count, dtype=jnp.int32)[None, :]).astype(
        jnp.int32
    )
    running = jnp.cumsum(onehot, axis=0)
    slot_index = flat_expert * cap + jnp.sum((running - 1) * onehot, axis=1)
    slot_total = pair_count * cap
    source_token = (
        jnp.zeros((slot_total,), jnp.int32)
        .at[slot_index]
        .set(jnp.arange(route_total, dtype=jnp.int32) // TOP)
    )
    filled = jnp.zeros((slot_total,), jnp.bool_).at[slot_index].set(True)
    return slot_index, source_token, filled


def by_slots(tokens, grad_out, routes, route_weights, gate_weight, up_weight, down_weight):
    group_count = lax.axis_size("grp")
    rank_count = lax.axis_size("ep")
    pair_count = group_count // 2
    both = ("grp", "ep")
    group_tokens, width = tokens.shape
    per_device = group_tokens // rank_count
    slots = 2 * ((per_device * TOP + 2 * pair_count - 1) // (2 * pair_count))
    cap = rank_count * slots
    extra = LANES
    slot_index, source_token, filled = slot_tables(routes, pair_count, cap)

    paired = jnp.concatenate([tokens, grad_out], axis=1)
    packed = jnp.where(filled[:, None], paired[source_token], jnp.zeros((), paired.dtype))
    send = packed.reshape(1, pair_count, rank_count, slots, 2 * width)
    send = jnp.broadcast_to(send, (2,) + send.shape[1:])
    send = send.reshape(group_count * rank_count, slots, 2 * width)
    held = lax.all_to_all(send, both, split_axis=0, concat_axis=0, tiled=True)
    held = held.reshape(group_count, rank_count, slots, 2, width)
    held = held.transpose(3, 0, 2, 1, 4).reshape(2, group_count * slots, rank_count * width)
    gate_pre = times_rows(held[0], gate_weight[0])
    up_pre = times_rows(held[0], up_weight[0])
    back_proj = times_rows(held[1], down_weight[0])
    product, grad_gate_pre, grad_up_pre = gradients(gate_pre, up_pre, back_proj)
    inner_sum = jnp.sum(product, axis=1, keepdims=True)
    partial = times_units(grad_gate_pre, gate_weight[0]) + times_units(grad_up_pre, up_weight[0])
    back = partial.astype(jnp.bfloat16).reshape(group_count, slots, rank_count, width)
    back = back.transpose(0, 2, 1, 3)
    parts = jnp.concatenate(split_float(inner_sum), axis=1).astype(jnp.bfloat16)
    parts = jnp.pad(parts, ((0, 0), (0, extra - PARTS))).reshape(group_count, 1, slots, extra)
    parts = jnp.broadcast_to(parts, (group_count, rank_count, slots, extra))
    back = jnp.concatenate([back, parts], axis=-1)
    back = back.reshape(group_count * rank_count, slots, width + extra)
    arrived = lax.all_to_all(back, both, split_axis=0, concat_axis=0, tiled=True)
    arrived = arrived.reshape(2, pair_count * cap, width + extra).astype(jnp.float32)
    per_route = (arrived[0] + arrived[1])[slot_index].reshape(group_tokens, TOP, width + extra)
    grad_tokens = jnp.sum(per_route[..., :width] * route_weights[:, :, None], axis=1)
    grad_gates = jnp.sum(per_route[..., width : width + PARTS], axis=2)
    return (grad_tokens.astype(jnp.bfloat16), grad_gates)


def on_device(*args):
    everywhere = lax.axis_size("grp") // 2 == TOP and args[0].shape[0] == LANES
    everywhere = everywhere and lax.axis_size("ep") % 2 == 0
    return every_expert(*args) if everywhere else by_slots(*args)


def solution(mesh):
    placed = (
        P("grp", "ep"),
        P("grp", "ep"),
        P("grp", None),
        P("grp", None),
        P("grp", None, None),
        P("grp", None, None),
        P("grp", None, None),
    )
    return jax.shard_map(
        on_device,
        mesh=mesh,
        in_specs=placed,
        out_specs=(P("grp", "ep"), P("grp", None)),
        check_vma=False,
    )
```

```python
import jax
import jax.numpy as jnp
from jax import lax
from jax.experimental import pallas as pl
from jax.experimental.pallas import tpu as pltpu
from jax.sharding import PartitionSpec as P

TOP = 2
LANES = 128
PARTS = 2
TILE = 256
VMEM_BYTES = 40 * 1024 * 1024


def gradients(gate_pre, up_pre, back_proj):
    sigmoid_gate = jax.nn.sigmoid(gate_pre)
    active = gate_pre * sigmoid_gate
    hidden = (active * up_pre).astype(jnp.bfloat16)
    product = hidden.astype(jnp.float32) * back_proj
    grad_gate_pre = back_proj * up_pre * sigmoid_gate * (1.0 + gate_pre * (1.0 - sigmoid_gate))
    grad_up_pre = back_proj * active
    return product, grad_gate_pre.astype(jnp.bfloat16), grad_up_pre.astype(jnp.bfloat16)


def times_rows(rows, weight):
    contract = (((1,), (1,)), ((), ()))
    return lax.dot_general(rows, weight, contract, preferred_element_type=jnp.float32)


def times_units(grads, weight):
    return jnp.dot(grads, weight, preferred_element_type=jnp.float32)


def split_float(value):
    first = value.astype(jnp.bfloat16).astype(jnp.float32)
    second = (value - first).astype(jnp.bfloat16).astype(jnp.float32)
    return first, second


def repeat_lanes(row, start, count):
    lane = lax.broadcasted_iota(jnp.int32, row.shape, 1)
    row = jnp.where((lane >= start) & (lane < start + count), row, 0.0)
    row = pltpu.roll(row, (LANES - start) % LANES, 1)
    while count < LANES:
        row = row + pltpu.roll(row, count, 1)
        count *= 2
    return row


def half_kernel(rows_ref, gate_ref, up_ref, down_ref, out_ref):
    rank_count, group_count, slots, width = rows_ref.shape
    width = width // 2
    total = group_count * slots
    slices = [slice(rank * width, (rank + 1) * width) for rank in range(rank_count)]

    units = gate_ref.shape[1]
    cut = units // TILE * TILE
    main, rest = slice(0, cut), slice(cut, units)

    first, second = slice(0, width), slice(width, 2 * width)
    gate_main = up_main = both_rest = turned = 0.0
    for rank, columns in enumerate(slices):
        rows_in = rows_ref[rank, :, :, first].reshape(total, width)
        rows_back = rows_ref[rank, :, :, second].reshape(total, width)
        both = jnp.concatenate([gate_ref[0, rest, columns], up_ref[0, rest, columns]], axis=0)
        turned = turned + times_rows(down_ref[0, :, columns], rows_back)
        gate_main = gate_main + times_rows(rows_in, gate_ref[0, main, columns])
        up_main = up_main + times_rows(rows_in, up_ref[0, main, columns])
        both_rest = both_rest + times_rows(rows_in, both)
    back_proj = jnp.concatenate([turned, jnp.zeros((units, LANES - total), jnp.float32)], axis=1).T[:total]
    back_main, back_rest = back_proj[:, main], back_proj[:, rest]
    product_main, by_gate_main, by_up_main = gradients(gate_main, up_main, back_main)
    product_rest, by_gate_rest, by_up_rest = gradients(
        both_rest[:, : units - cut], both_rest[:, units - cut :], back_rest
    )
    product = jnp.concatenate([product_main, product_rest], axis=1)
    by_rest = jnp.concatenate([by_gate_rest, by_up_rest], axis=1)

    folded = product[:, :LANES]
    for start in range(LANES, product.shape[1], LANES):
        folded = folded + product[:, start : start + LANES]
    folded = jnp.concatenate([folded, jnp.zeros((LANES - total, LANES), jnp.float32)], axis=0)
    inner_sum = jnp.sum(folded.T, axis=0, keepdims=True)
    line = lax.broadcasted_iota(jnp.int32, (2, LANES), 0)
    for group in range(group_count):
        tail = jnp.zeros((2, LANES), jnp.float32)
        for index, piece in enumerate(split_float(repeat_lanes(inner_sum, group * slots, slots))):
            tail = jnp.where(line == index, piece, tail)
        for rank in range(rank_count):
            out_ref[rank, group, slots * (width // LANES) // 2] = tail.astype(jnp.bfloat16)

    for rank, columns in enumerate(slices):
        weight_rest = jnp.concatenate([gate_ref[0, rest, columns], up_ref[0, rest, columns]], axis=0)
        partial = times_units(by_gate_main, gate_ref[0, main, columns])
        partial = partial + times_units(by_up_main, up_ref[0, main, columns])
        partial = partial + times_units(by_rest, weight_rest)
        partial = partial.astype(jnp.bfloat16)
        for group in range(group_count):
            rows = slice(group * slots, (group + 1) * slots)
            for index in range(width // LANES):
                lanes = slice(index * LANES, (index + 1) * LANES)
                place = slice(index * slots // 2, (index + 1) * slots // 2)
                out_ref[rank, group, place] = partial[rows, lanes].reshape(slots // 2, 2, LANES)


def owner_kernel(parts_ref, routes_ref, weights_ref, grad_ref, gates_ref):
    rank_count, _, length, _, _ = parts_ref.shape
    total, width = grad_ref.shape
    slots = total // rank_count
    body = slots * (width // LANES) // 2
    first = routes_ref[:1, :] == 0
    scale_first = jnp.where(first, weights_ref[:1, :], weights_ref[1:, :])
    scale_second = jnp.where(first, weights_ref[1:, :], weights_ref[:1, :])
    line = lax.broadcasted_iota(jnp.int32, (LANES, total), 0)
    turned = jnp.where(line == 0, scale_first, scale_second).T
    scales = (turned[:, :1], turned[:, 1:2])
    for rank in range(rank_count):
        rows = slice(rank * slots, (rank + 1) * slots)
        for index in range(width // LANES):
            place = slice(index * slots // 2, (index + 1) * slots // 2)
            value = 0.0
            for expert in range(TOP):
                pair = parts_ref[rank, expert, place].astype(jnp.float32)
                pair = pair + parts_ref[rank, expert + TOP, place].astype(jnp.float32)
                value = value + scales[expert][rows] * pair.reshape(slots, LANES)
            grad_ref[rows, index * LANES : (index + 1) * LANES] = value.astype(jnp.bfloat16)
    owner = lax.broadcasted_iota(jnp.int32, (2, LANES), 1) // slots
    inner = []
    for expert in range(TOP):
        value = jnp.zeros((2, LANES), jnp.float32)
        for rank in range(rank_count):
            pair = parts_ref[rank, expert, body].astype(jnp.float32)
            pair = pair + parts_ref[rank, expert + TOP, body].astype(jnp.float32)
            value = value + jnp.where(owner == rank, pair, 0.0)
        inner.append(jnp.sum(value, axis=0, keepdims=True))
    gates_ref[...] = jnp.where(routes_ref[...] == 0, inner[0], inner[1])


def every_expert(tokens, grad_out, routes, route_weights, gate_weight, up_weight, down_weight):
    group_count = lax.axis_size("grp")
    rank_count = lax.axis_size("ep")
    both = ("ep", "grp")
    group_tokens, width = tokens.shape
    slots = group_tokens // rank_count
    length = slots * (width // LANES) // 2 + 1
    whole = pl.BlockSpec(memory_space=pltpu.VMEM)
    params = pltpu.CompilerParams(vmem_limit_bytes=VMEM_BYTES)

    paired = jnp.concatenate([tokens, grad_out], axis=1).reshape(rank_count, 1, slots, 2 * width)
    send = jnp.broadcast_to(paired, (rank_count, group_count, slots, 2 * width))
    swap = [(source, source ^ 1) for source in range(rank_count)]
    send, up_weight, down_weight = lax.optimization_barrier((send, up_weight, down_weight))
    up_weight = lax.ppermute(up_weight, "ep", swap)
    down_weight = lax.ppermute(down_weight, "ep", swap)
    send = send.reshape(group_count * rank_count, slots, 2 * width)
    held = lax.all_to_all(send, both, split_axis=0, concat_axis=0, tiled=True)
    back = pl.pallas_call(
        half_kernel,
        out_shape=jax.ShapeDtypeStruct((rank_count, group_count, length, 2, LANES), jnp.bfloat16),
        in_specs=[whole] * 4,
        out_specs=whole,
        compiler_params=params,
    )(
        held.reshape(rank_count, group_count, slots, 2 * width),
        gate_weight,
        up_weight,
        down_weight,
    )
    back = back.reshape(group_count * rank_count, length, 2, LANES)
    arrived = lax.all_to_all(back, both, split_axis=0, concat_axis=0, tiled=True)
    grad_tokens, grad_gates = pl.pallas_call(
        owner_kernel,
        out_shape=(
            jax.ShapeDtypeStruct(tokens.shape, jnp.bfloat16),
            jax.ShapeDtypeStruct((TOP, group_tokens), jnp.float32),
        ),
        in_specs=[whole] * 3,
        out_specs=(whole, whole),
        compiler_params=params,
    )(arrived.reshape(rank_count, group_count, length, 2, LANES), routes.T, route_weights.T)
    return grad_tokens, grad_gates.T


def slot_tables(routes, pair_count, cap):
    flat_expert = routes.reshape(-1)
    route_total = flat_expert.shape[0]
    onehot = (flat_expert[:, None] == jnp.arange(pair_count, dtype=jnp.int32)[None, :]).astype(
        jnp.int32
    )
    running = jnp.cumsum(onehot, axis=0)
    slot_index = flat_expert * cap + jnp.sum((running - 1) * onehot, axis=1)
    slot_total = pair_count * cap
    source_token = (
        jnp.zeros((slot_total,), jnp.int32)
        .at[slot_index]
        .set(jnp.arange(route_total, dtype=jnp.int32) // TOP)
    )
    filled = jnp.zeros((slot_total,), jnp.bool_).at[slot_index].set(True)
    return slot_index, source_token, filled


def by_slots(tokens, grad_out, routes, route_weights, gate_weight, up_weight, down_weight):
    group_count = lax.axis_size("grp")
    rank_count = lax.axis_size("ep")
    pair_count = group_count // 2
    both = ("grp", "ep")
    group_tokens, width = tokens.shape
    per_device = group_tokens // rank_count
    slots = 2 * ((per_device * TOP + 2 * pair_count - 1) // (2 * pair_count))
    cap = rank_count * slots
    extra = LANES
    slot_index, source_token, filled = slot_tables(routes, pair_count, cap)

    paired = jnp.concatenate([tokens, grad_out], axis=1)
    packed = jnp.where(filled[:, None], paired[source_token], jnp.zeros((), paired.dtype))
    send = packed.reshape(1, pair_count, rank_count, slots, 2 * width)
    send = jnp.broadcast_to(send, (2,) + send.shape[1:])
    send = send.reshape(group_count * rank_count, slots, 2 * width)
    held = lax.all_to_all(send, both, split_axis=0, concat_axis=0, tiled=True)
    held = held.reshape(group_count, rank_count, slots, 2, width)
    held = held.transpose(3, 0, 2, 1, 4).reshape(2, group_count * slots, rank_count * width)
    gate_pre = times_rows(held[0], gate_weight[0])
    up_pre = times_rows(held[0], up_weight[0])
    back_proj = times_rows(held[1], down_weight[0])
    product, grad_gate_pre, grad_up_pre = gradients(gate_pre, up_pre, back_proj)
    inner_sum = jnp.sum(product, axis=1, keepdims=True)
    partial = times_units(grad_gate_pre, gate_weight[0]) + times_units(grad_up_pre, up_weight[0])
    back = partial.astype(jnp.bfloat16).reshape(group_count, slots, rank_count, width)
    back = back.transpose(0, 2, 1, 3)
    parts = jnp.concatenate(split_float(inner_sum), axis=1).astype(jnp.bfloat16)
    parts = jnp.pad(parts, ((0, 0), (0, extra - PARTS))).reshape(group_count, 1, slots, extra)
    parts = jnp.broadcast_to(parts, (group_count, rank_count, slots, extra))
    back = jnp.concatenate([back, parts], axis=-1)
    back = back.reshape(group_count * rank_count, slots, width + extra)
    arrived = lax.all_to_all(back, both, split_axis=0, concat_axis=0, tiled=True)
    arrived = arrived.reshape(2, pair_count * cap, width + extra).astype(jnp.float32)
    per_route = (arrived[0] + arrived[1])[slot_index].reshape(group_tokens, TOP, width + extra)
    grad_tokens = jnp.sum(per_route[..., :width] * route_weights[:, :, None], axis=1)
    grad_gates = jnp.sum(per_route[..., width : width + PARTS], axis=2)
    return (grad_tokens.astype(jnp.bfloat16), grad_gates)


def on_device(*args):
    everywhere = lax.axis_size("grp") // 2 == TOP and args[0].shape[0] == LANES
    everywhere = everywhere and lax.axis_size("ep") % 2 == 0
    return every_expert(*args) if everywhere else by_slots(*args)


def solution(mesh):
    placed = (
        P("grp", "ep"),
        P("grp", "ep"),
        P("grp", None),
        P("grp", None),
        P("grp", None, None),
        P("grp", None, None),
        P("grp", None, None),
    )
    return jax.shard_map(
        on_device,
        mesh=mesh,
        in_specs=placed,
        out_specs=(P("grp", "ep"), P("grp", None)),
        check_vma=False,
    )
```

```python
import functools
import math

import jax
import jax.numpy as jnp
import numpy as np
from jax import lax
from jax.experimental import pallas as pl
from jax.experimental.pallas import tpu as pltpu
from jax.sharding import Mesh
from jax.sharding import PartitionSpec as P

TOP = 2
LANES = 128
PARTS = 2
TILE = 256
RANK_AXES = ("ep_y", "ep_x", "ep_core")
GROUP_AXES = ("grp_hi", "grp_lo")
SEND_AXES = ("ep_x", "ep_y", "grp_hi", "ep_core", "grp_lo")
VMEM_BYTES = 40 * 1024 * 1024


def gradients(gate_pre, up_pre, back_proj):
    sigmoid_gate = jax.nn.sigmoid(gate_pre)
    active = gate_pre * sigmoid_gate
    hidden = (active * up_pre).astype(jnp.bfloat16)
    product = hidden.astype(jnp.float32) * back_proj
    grad_gate_pre = back_proj * up_pre * sigmoid_gate * (1.0 + gate_pre * (1.0 - sigmoid_gate))
    grad_up_pre = back_proj * active
    return product, grad_gate_pre.astype(jnp.bfloat16), grad_up_pre.astype(jnp.bfloat16)


def times_rows(rows, weight):
    contract = (((1,), (1,)), ((), ()))
    return lax.dot_general(rows, weight, contract, preferred_element_type=jnp.float32)


def times_units(grads, weight):
    return jnp.dot(grads, weight, preferred_element_type=jnp.float32)


def split_float(value):
    first = value.astype(jnp.bfloat16).astype(jnp.float32)
    second = (value - first).astype(jnp.bfloat16).astype(jnp.float32)
    return first, second


def repeat_lanes(row, start, count):
    lane = lax.broadcasted_iota(jnp.int32, row.shape, 1)
    row = jnp.where((lane >= start) & (lane < start + count), row, 0.0)
    row = pltpu.roll(row, (LANES - start) % LANES, 1)
    while count < LANES:
        row = row + pltpu.roll(row, count, 1)
        count *= 2
    return row


def pack_kernel(places, tokens_hbm, grad_hbm, out_ref, tokens_ref, grad_ref, arrived):
    _, slots, width = out_ref.shape
    lanes = (slice(0, width // 2), slice(width // 2, width))
    copies = [
        pltpu.make_async_copy(tokens_hbm, tokens_ref, arrived.at[0]),
        pltpu.make_async_copy(grad_hbm, grad_ref, arrived.at[1]),
    ]
    for copy in copies:
        copy.start()
    for copy, source, half in zip(copies, (tokens_ref, grad_ref), lanes):
        copy.wait()
        for of_group in places:
            for rank, place in enumerate(of_group):
                out_ref[place, :, half] = source[rank * slots : (rank + 1) * slots, :]


def half_kernel(places, rows_ref, gate_ref, up_ref, down_ref, out_ref):
    group_count, rank_count = len(places), len(places[0])
    _, slots, width = rows_ref.shape
    width = width // 2
    total = group_count * slots
    slices = [slice(rank * width, (rank + 1) * width) for rank in range(rank_count)]
    units = gate_ref.shape[1]
    cut = units // TILE * TILE
    main, rest = slice(0, cut), slice(cut, units)

    first, second = slice(0, width), slice(width, 2 * width)
    gate_main = up_main = both_rest = turned = 0.0
    for rank, columns in enumerate(slices):
        rows_in = jnp.concatenate([rows_ref[of_group[rank], :, first] for of_group in places], axis=0)
        rows_back = jnp.concatenate([rows_ref[of_group[rank], :, second] for of_group in places], axis=0)
        both = jnp.concatenate([gate_ref[0, rest, columns], up_ref[0, rest, columns]], axis=0)
        turned = turned + times_rows(down_ref[0, :, columns], rows_back)
        gate_main = gate_main + times_rows(rows_in, gate_ref[0, main, columns])
        up_main = up_main + times_rows(rows_in, up_ref[0, main, columns])
        both_rest = both_rest + times_rows(rows_in, both)
    back_proj = jnp.concatenate([turned, jnp.zeros((units, LANES - total), jnp.float32)], axis=1).T[:total]
    back_main, back_rest = back_proj[:, main], back_proj[:, rest]
    product_main, by_gate_main, by_up_main = gradients(gate_main, up_main, back_main)
    product_rest, by_gate_rest, by_up_rest = gradients(
        both_rest[:, : units - cut], both_rest[:, units - cut :], back_rest
    )
    product = jnp.concatenate([product_main, product_rest], axis=1)
    by_rest = jnp.concatenate([by_gate_rest, by_up_rest], axis=1)

    folded = product[:, :LANES]
    for start in range(LANES, product.shape[1], LANES):
        folded = folded + product[:, start : start + LANES]
    folded = jnp.concatenate([folded, jnp.zeros((LANES - total, LANES), jnp.float32)], axis=0)
    inner_sum = jnp.sum(folded.T, axis=0, keepdims=True)
    line = lax.broadcasted_iota(jnp.int32, (2, LANES), 0)
    for group in range(group_count):
        tail = jnp.zeros((2, LANES), jnp.float32)
        for index, piece in enumerate(split_float(repeat_lanes(inner_sum, group * slots, slots))):
            tail = jnp.where(line == index, piece, tail)
        for place in places[group]:
            out_ref[place, slots * (width // LANES) // 2] = tail.astype(jnp.bfloat16)

    for rank, columns in enumerate(slices):
        weight_rest = jnp.concatenate([gate_ref[0, rest, columns], up_ref[0, rest, columns]], axis=0)
        partial = times_units(by_gate_main, gate_ref[0, main, columns])
        partial = partial + times_units(by_up_main, up_ref[0, main, columns])
        partial = partial + times_units(by_rest, weight_rest)
        partial = partial.astype(jnp.bfloat16)
        for group in range(group_count):
            rows = slice(group * slots, (group + 1) * slots)
            for index in range(width // LANES):
                lanes = slice(index * LANES, (index + 1) * LANES)
                pairs = slice(index * slots // 2, (index + 1) * slots // 2)
                out_ref[places[group][rank], pairs] = partial[rows, lanes].reshape(slots // 2, 2, LANES)


def owner_kernel(places, parts_ref, routes_ref, weights_ref, grad_ref, gates_ref):
    count, length, _, _ = parts_ref.shape
    total, width = grad_ref.shape
    slots = total // len(places[0])
    body = slots * (width // LANES) // 2
    first = routes_ref[:1, :] == 0
    scale_first = jnp.where(first, weights_ref[:1, :], weights_ref[1:, :])
    scale_second = jnp.where(first, weights_ref[1:, :], weights_ref[:1, :])
    line = lax.broadcasted_iota(jnp.int32, (LANES, total), 0)
    turned = jnp.where(line == 0, scale_first, scale_second).T
    scales = (turned[:, :1], turned[:, 1:2])
    for rank in range(len(places[0])):
        rows = slice(rank * slots, (rank + 1) * slots)
        for index in range(width // LANES):
            pairs = slice(index * slots // 2, (index + 1) * slots // 2)
            value = 0.0
            for expert in range(TOP):
                pair = parts_ref[places[expert][rank], pairs].astype(jnp.float32)
                pair = pair + parts_ref[places[expert + TOP][rank], pairs].astype(jnp.float32)
                value = value + scales[expert][rows] * pair.reshape(slots, LANES)
            grad_ref[rows, index * LANES : (index + 1) * LANES] = value.astype(jnp.bfloat16)
    owner = lax.broadcasted_iota(jnp.int32, (2, LANES), 1) // slots
    inner = []
    for expert in range(TOP):
        value = jnp.zeros((2, LANES), jnp.float32)
        for rank in range(len(places[0])):
            pair = parts_ref[places[expert][rank], body].astype(jnp.float32)
            pair = pair + parts_ref[places[expert + TOP][rank], body].astype(jnp.float32)
            value = value + jnp.where(owner == rank, pair, 0.0)
        inner.append(jnp.sum(value, axis=0, keepdims=True))
    gates_ref[...] = jnp.where(routes_ref[...] == 0, inner[0], inner[1])


def message_places(order):
    axes = GROUP_AXES + RANK_AXES
    sizes = [lax.axis_size(axis) for axis in axes]
    linear = np.arange(math.prod(sizes)).reshape([lax.axis_size(axis) for axis in order])
    linear = linear.transpose([order.index(axis) for axis in axes])
    return linear.reshape(sizes[0] * sizes[1], -1).tolist()


def every_expert(tokens, grad_out, routes, route_weights, gate_weight, up_weight, down_weight):
    rank_count = lax.axis_size(RANK_AXES)
    count = lax.axis_size(SEND_AXES)
    group_tokens, width = tokens.shape
    slots = group_tokens // rank_count
    length = slots * (width // LANES) // 2 + 1
    whole = pl.BlockSpec(memory_space=pltpu.VMEM)
    there = pl.BlockSpec(memory_space=pltpu.HBM)
    params = pltpu.CompilerParams(vmem_limit_bytes=VMEM_BYTES)
    places = message_places(SEND_AXES)

    send = pl.pallas_call(
        functools.partial(pack_kernel, places),
        out_shape=jax.ShapeDtypeStruct((count, slots, 2 * width), tokens.dtype),
        in_specs=[there] * 2,
        out_specs=whole,
        scratch_shapes=[
            pltpu.VMEM(tokens.shape, tokens.dtype),
            pltpu.VMEM(tokens.shape, tokens.dtype),
            pltpu.SemaphoreType.DMA((2,)),
        ],
        compiler_params=params,
    )(*[pltpu.with_memory_space_constraint(value, pltpu.HBM) for value in (tokens, grad_out)])
    send, up_weight, down_weight = lax.optimization_barrier((send, up_weight, down_weight))
    up_weight = lax.ppermute(up_weight, RANK_AXES[-1], [(0, 1), (1, 0)])
    down_weight = lax.ppermute(down_weight, RANK_AXES[-1], [(0, 1), (1, 0)])
    held = lax.all_to_all(send, SEND_AXES, split_axis=0, concat_axis=0, tiled=True)
    back = pl.pallas_call(
        functools.partial(half_kernel, places),
        out_shape=jax.ShapeDtypeStruct((count, length, 2, LANES), jnp.bfloat16),
        in_specs=[whole] * 4,
        out_specs=whole,
        compiler_params=params,
    )(
        held,
        gate_weight,
        up_weight,
        down_weight,
    )
    arrived = lax.all_to_all(back, SEND_AXES, split_axis=0, concat_axis=0, tiled=True)
    grad_tokens, grad_gates = pl.pallas_call(
        functools.partial(owner_kernel, places),
        out_shape=(
            jax.ShapeDtypeStruct(tokens.shape, jnp.bfloat16),
            jax.ShapeDtypeStruct((TOP, group_tokens), jnp.float32),
        ),
        in_specs=[whole] * 3,
        out_specs=(whole, whole),
        compiler_params=params,
    )(arrived, routes.T, route_weights.T)
    return grad_tokens, grad_gates.T


def slot_tables(routes, pair_count, cap):
    flat_expert = routes.reshape(-1)
    route_total = flat_expert.shape[0]
    onehot = (flat_expert[:, None] == jnp.arange(pair_count, dtype=jnp.int32)[None, :]).astype(
        jnp.int32
    )
    running = jnp.cumsum(onehot, axis=0)
    slot_index = flat_expert * cap + jnp.sum((running - 1) * onehot, axis=1)
    slot_total = pair_count * cap
    source_token = (
        jnp.zeros((slot_total,), jnp.int32)
        .at[slot_index]
        .set(jnp.arange(route_total, dtype=jnp.int32) // TOP)
    )
    filled = jnp.zeros((slot_total,), jnp.bool_).at[slot_index].set(True)
    return slot_index, source_token, filled


def by_slots(tokens, grad_out, routes, route_weights, gate_weight, up_weight, down_weight):
    group_count = lax.axis_size("grp")
    rank_count = lax.axis_size("ep")
    pair_count = group_count // 2
    both = ("grp", "ep")
    group_tokens, width = tokens.shape
    per_device = group_tokens // rank_count
    slots = 2 * ((per_device * TOP + 2 * pair_count - 1) // (2 * pair_count))
    cap = rank_count * slots
    extra = LANES
    slot_index, source_token, filled = slot_tables(routes, pair_count, cap)

    paired = jnp.concatenate([tokens, grad_out], axis=1)
    packed = jnp.where(filled[:, None], paired[source_token], jnp.zeros((), paired.dtype))
    send = packed.reshape(1, pair_count, rank_count, slots, 2 * width)
    send = jnp.broadcast_to(send, (2,) + send.shape[1:])
    send = send.reshape(group_count * rank_count, slots, 2 * width)
    held = lax.all_to_all(send, both, split_axis=0, concat_axis=0, tiled=True)
    held = held.reshape(group_count, rank_count, slots, 2, width)
    held = held.transpose(3, 0, 2, 1, 4).reshape(2, group_count * slots, rank_count * width)
    gate_pre = times_rows(held[0], gate_weight[0])
    up_pre = times_rows(held[0], up_weight[0])
    back_proj = times_rows(held[1], down_weight[0])
    product, grad_gate_pre, grad_up_pre = gradients(gate_pre, up_pre, back_proj)
    inner_sum = jnp.sum(product, axis=1, keepdims=True)
    partial = times_units(grad_gate_pre, gate_weight[0]) + times_units(grad_up_pre, up_weight[0])
    back = partial.astype(jnp.bfloat16).reshape(group_count, slots, rank_count, width)
    back = back.transpose(0, 2, 1, 3)
    parts = jnp.concatenate(split_float(inner_sum), axis=1).astype(jnp.bfloat16)
    parts = jnp.pad(parts, ((0, 0), (0, extra - PARTS))).reshape(group_count, 1, slots, extra)
    parts = jnp.broadcast_to(parts, (group_count, rank_count, slots, extra))
    back = jnp.concatenate([back, parts], axis=-1)
    back = back.reshape(group_count * rank_count, slots, width + extra)
    arrived = lax.all_to_all(back, both, split_axis=0, concat_axis=0, tiled=True)
    arrived = arrived.reshape(2, pair_count * cap, width + extra).astype(jnp.float32)
    per_route = (arrived[0] + arrived[1])[slot_index].reshape(group_tokens, TOP, width + extra)
    grad_tokens = jnp.sum(per_route[..., :width] * route_weights[:, :, None], axis=1)
    grad_gates = jnp.sum(per_route[..., width : width + PARTS], axis=2)
    return (grad_tokens.astype(jnp.bfloat16), grad_gates)


def solution(mesh):
    groups, ranks = mesh.shape["grp"], mesh.shape["ep"]

    def run(tokens, *others):
        everywhere = groups == 2 * TOP and tokens.shape[0] == groups * LANES and ranks == 8
        if everywhere:
            fine = Mesh(mesh.devices.reshape([2] * 5), GROUP_AXES + RANK_AXES)
            placed, body, axes, grp = fine, every_expert, RANK_AXES, GROUP_AXES
        else:
            placed, body, axes, grp = mesh, by_slots, "ep", "grp"
        weights = [P(grp, None, None)] * 3
        return jax.shard_map(
            body,
            mesh=placed,
            in_specs=(P(grp, axes), P(grp, axes), P(grp, None), P(grp, None), *weights),
            out_specs=(P(grp, axes), P(grp, None)),
            check_vma=False,
        )(tokens, *others)

    return run
```

```python
import functools
import math

import jax
import jax.numpy as jnp
import numpy as np
from jax import lax
from jax.experimental import pallas as pl
from jax.experimental.pallas import tpu as pltpu
from jax.sharding import Mesh
from jax.sharding import PartitionSpec as P

TOP = 2
LANES = 128
PARTS = 2
TILE = 256
RANK_AXES = ("ep_y", "ep_x", "ep_core")
GROUP_AXES = ("grp_hi", "grp_lo")
SEND_AXES = ("ep_x", "ep_y", "grp_hi", "ep_core", "grp_lo")
VMEM_BYTES = 40 * 1024 * 1024


def gradients(gate_pre, up_pre, back_proj):
    sigmoid_gate = jax.nn.sigmoid(gate_pre)
    active = gate_pre * sigmoid_gate
    hidden = (active * up_pre).astype(jnp.bfloat16)
    product = hidden.astype(jnp.float32) * back_proj
    grad_gate_pre = back_proj * up_pre * sigmoid_gate * (1.0 + gate_pre * (1.0 - sigmoid_gate))
    grad_up_pre = back_proj * active
    return product, grad_gate_pre.astype(jnp.bfloat16), grad_up_pre.astype(jnp.bfloat16)


def times_rows(rows, weight):
    contract = (((1,), (1,)), ((), ()))
    return lax.dot_general(rows, weight, contract, preferred_element_type=jnp.float32)


def times_units(grads, weight):
    return jnp.dot(grads, weight, preferred_element_type=jnp.float32)


def split_float(value):
    first = value.astype(jnp.bfloat16).astype(jnp.float32)
    second = (value - first).astype(jnp.bfloat16).astype(jnp.float32)
    return first, second


def repeat_lanes(row, start, count):
    lane = lax.broadcasted_iota(jnp.int32, row.shape, 1)
    row = jnp.where((lane >= start) & (lane < start + count), row, 0.0)
    row = pltpu.roll(row, (LANES - start) % LANES, 1)
    while count < LANES:
        row = row + pltpu.roll(row, count, 1)
        count *= 2
    return row


def pack_kernel(places, tokens_hbm, grad_hbm, out_ref, tokens_ref, grad_ref, arrived):
    _, slots, width = out_ref.shape
    lanes = (slice(0, width // 2), slice(width // 2, width))
    copies = [
        pltpu.make_async_copy(tokens_hbm, tokens_ref, arrived.at[0]),
        pltpu.make_async_copy(grad_hbm, grad_ref, arrived.at[1]),
    ]
    for copy in copies:
        copy.start()
    for copy, source, half in zip(copies, (tokens_ref, grad_ref), lanes):
        copy.wait()
        for of_group in places:
            for rank, place in enumerate(of_group):
                out_ref[place, :, half] = source[rank * slots : (rank + 1) * slots, :]


def half_kernel(places, rows_ref, gate_ref, up_ref, down_ref, out_ref):
    group_count, rank_count = len(places), len(places[0])
    _, slots, width = rows_ref.shape
    width = width // 2
    total = group_count * slots
    slices = [slice(rank * width, (rank + 1) * width) for rank in range(rank_count)]
    units = gate_ref.shape[1]
    cut = units // TILE * TILE
    main, rest = slice(0, cut), slice(cut, units)

    gate_main = up_main = both_rest = turned = 0.0
    for at in range(0, rank_count * width, TILE):
        rank, start = divmod(at, width)
        columns = slice(at, at + TILE)
        first, second = slice(start, start + TILE), slice(width + start, width + start + TILE)
        rows_in = jnp.concatenate([rows_ref[of_group[rank], :, first] for of_group in places], axis=0)
        rows_back = jnp.concatenate([rows_ref[of_group[rank], :, second] for of_group in places], axis=0)
        both = jnp.concatenate([gate_ref[0, rest, columns], up_ref[0, rest, columns]], axis=0)
        gate_main = gate_main + times_rows(rows_in, gate_ref[0, main, columns])
        turned = turned + times_rows(down_ref[0, :, columns], rows_back)
        up_main = up_main + times_rows(rows_in, up_ref[0, main, columns])
        both_rest = both_rest + times_rows(rows_in, both)
    back_proj = jnp.concatenate([turned, jnp.zeros((units, LANES - total), jnp.float32)], axis=1).T[:total]
    back_main, back_rest = back_proj[:, main], back_proj[:, rest]
    product_main, by_gate_main, by_up_main = gradients(gate_main, up_main, back_main)
    product_rest, by_gate_rest, by_up_rest = gradients(
        both_rest[:, : units - cut], both_rest[:, units - cut :], back_rest
    )
    product = jnp.concatenate([product_main, product_rest], axis=1)
    by_rest = jnp.concatenate([by_gate_rest, by_up_rest], axis=1)

    folded = product[:, :LANES]
    for start in range(LANES, product.shape[1], LANES):
        folded = folded + product[:, start : start + LANES]
    folded = jnp.concatenate([folded, jnp.zeros((LANES - total, LANES), jnp.float32)], axis=0)
    inner_sum = jnp.sum(folded.T, axis=0, keepdims=True)
    line = lax.broadcasted_iota(jnp.int32, (2, LANES), 0)
    for group in range(group_count):
        tail = jnp.zeros((2, LANES), jnp.float32)
        for index, piece in enumerate(split_float(repeat_lanes(inner_sum, group * slots, slots))):
            tail = jnp.where(line == index, piece, tail)
        for place in places[group]:
            out_ref[place, slots * (width // LANES) // 2] = tail.astype(jnp.bfloat16)

    for rank, columns in enumerate(slices):
        weight_rest = jnp.concatenate([gate_ref[0, rest, columns], up_ref[0, rest, columns]], axis=0)
        partial = times_units(by_gate_main, gate_ref[0, main, columns])
        partial = partial + times_units(by_up_main, up_ref[0, main, columns])
        partial = partial + times_units(by_rest, weight_rest)
        partial = partial.astype(jnp.bfloat16)
        for group in range(group_count):
            rows = slice(group * slots, (group + 1) * slots)
            for index in range(width // LANES):
                lanes = slice(index * LANES, (index + 1) * LANES)
                pairs = slice(index * slots // 2, (index + 1) * slots // 2)
                out_ref[places[group][rank], pairs] = partial[rows, lanes].reshape(slots // 2, 2, LANES)


def owner_kernel(places, parts_ref, routes_ref, weights_ref, grad_ref, gates_ref):
    count, length, _, _ = parts_ref.shape
    total, width = grad_ref.shape
    slots = total // len(places[0])
    body = slots * (width // LANES) // 2
    first = routes_ref[:1, :] == 0
    scale_first = jnp.where(first, weights_ref[:1, :], weights_ref[1:, :])
    scale_second = jnp.where(first, weights_ref[1:, :], weights_ref[:1, :])
    line = lax.broadcasted_iota(jnp.int32, (LANES, total), 0)
    turned = jnp.where(line == 0, scale_first, scale_second).T
    scales = (turned[:, :1], turned[:, 1:2])
    for rank in range(len(places[0])):
        rows = slice(rank * slots, (rank + 1) * slots)
        for index in range(width // LANES):
            pairs = slice(index * slots // 2, (index + 1) * slots // 2)
            value = 0.0
            for expert in range(TOP):
                pair = parts_ref[places[expert][rank], pairs].astype(jnp.float32)
                pair = pair + parts_ref[places[expert + TOP][rank], pairs].astype(jnp.float32)
                value = value + scales[expert][rows] * pair.reshape(slots, LANES)
            grad_ref[rows, index * LANES : (index + 1) * LANES] = value.astype(jnp.bfloat16)
    owner = lax.broadcasted_iota(jnp.int32, (2, LANES), 1) // slots
    inner = []
    for expert in range(TOP):
        value = jnp.zeros((2, LANES), jnp.float32)
        for rank in range(len(places[0])):
            pair = parts_ref[places[expert][rank], body].astype(jnp.float32)
            pair = pair + parts_ref[places[expert + TOP][rank], body].astype(jnp.float32)
            value = value + jnp.where(owner == rank, pair, 0.0)
        inner.append(jnp.sum(value, axis=0, keepdims=True))
    gates_ref[...] = jnp.where(routes_ref[...] == 0, inner[0], inner[1])


def message_places(order):
    axes = GROUP_AXES + RANK_AXES
    sizes = [lax.axis_size(axis) for axis in axes]
    linear = np.arange(math.prod(sizes)).reshape([lax.axis_size(axis) for axis in order])
    linear = linear.transpose([order.index(axis) for axis in axes])
    return linear.reshape(sizes[0] * sizes[1], -1).tolist()


def every_expert(tokens, grad_out, routes, route_weights, gate_weight, up_weight, down_weight):
    rank_count = lax.axis_size(RANK_AXES)
    count = lax.axis_size(SEND_AXES)
    group_tokens, width = tokens.shape
    slots = group_tokens // rank_count
    length = slots * (width // LANES) // 2 + 1
    whole = pl.BlockSpec(memory_space=pltpu.VMEM)
    there = pl.BlockSpec(memory_space=pltpu.HBM)
    params = pltpu.CompilerParams(vmem_limit_bytes=VMEM_BYTES)
    places = message_places(SEND_AXES)

    send = pl.pallas_call(
        functools.partial(pack_kernel, places),
        out_shape=jax.ShapeDtypeStruct((count, slots, 2 * width), tokens.dtype),
        in_specs=[there] * 2,
        out_specs=whole,
        scratch_shapes=[
            pltpu.VMEM(tokens.shape, tokens.dtype),
            pltpu.VMEM(tokens.shape, tokens.dtype),
            pltpu.SemaphoreType.DMA((2,)),
        ],
        compiler_params=params,
    )(*[pltpu.with_memory_space_constraint(value, pltpu.HBM) for value in (tokens, grad_out)])
    send, up_weight, down_weight = lax.optimization_barrier((send, up_weight, down_weight))
    up_weight = lax.ppermute(up_weight, RANK_AXES[-1], [(0, 1), (1, 0)])
    down_weight = lax.ppermute(down_weight, RANK_AXES[-1], [(0, 1), (1, 0)])
    held = lax.all_to_all(send, SEND_AXES, split_axis=0, concat_axis=0, tiled=True)
    back = pl.pallas_call(
        functools.partial(half_kernel, places),
        out_shape=jax.ShapeDtypeStruct((count, length, 2, LANES), jnp.bfloat16),
        in_specs=[whole] * 4,
        out_specs=whole,
        compiler_params=params,
    )(
        held,
        gate_weight,
        up_weight,
        down_weight,
    )
    arrived = lax.all_to_all(back, SEND_AXES, split_axis=0, concat_axis=0, tiled=True)
    grad_tokens, grad_gates = pl.pallas_call(
        functools.partial(owner_kernel, places),
        out_shape=(
            jax.ShapeDtypeStruct(tokens.shape, jnp.bfloat16),
            jax.ShapeDtypeStruct((TOP, group_tokens), jnp.float32),
        ),
        in_specs=[whole] * 3,
        out_specs=(whole, whole),
        compiler_params=params,
    )(arrived, routes.T, route_weights.T)
    return grad_tokens, grad_gates.T


def slot_tables(routes, pair_count, cap):
    flat_expert = routes.reshape(-1)
    route_total = flat_expert.shape[0]
    onehot = (flat_expert[:, None] == jnp.arange(pair_count, dtype=jnp.int32)[None, :]).astype(
        jnp.int32
    )
    running = jnp.cumsum(onehot, axis=0)
    slot_index = flat_expert * cap + jnp.sum((running - 1) * onehot, axis=1)
    slot_total = pair_count * cap
    source_token = (
        jnp.zeros((slot_total,), jnp.int32)
        .at[slot_index]
        .set(jnp.arange(route_total, dtype=jnp.int32) // TOP)
    )
    filled = jnp.zeros((slot_total,), jnp.bool_).at[slot_index].set(True)
    return slot_index, source_token, filled


def by_slots(tokens, grad_out, routes, route_weights, gate_weight, up_weight, down_weight):
    group_count = lax.axis_size("grp")
    rank_count = lax.axis_size("ep")
    pair_count = group_count // 2
    both = ("grp", "ep")
    group_tokens, width = tokens.shape
    per_device = group_tokens // rank_count
    slots = 2 * ((per_device * TOP + 2 * pair_count - 1) // (2 * pair_count))
    cap = rank_count * slots
    extra = LANES
    slot_index, source_token, filled = slot_tables(routes, pair_count, cap)

    paired = jnp.concatenate([tokens, grad_out], axis=1)
    packed = jnp.where(filled[:, None], paired[source_token], jnp.zeros((), paired.dtype))
    send = packed.reshape(1, pair_count, rank_count, slots, 2 * width)
    send = jnp.broadcast_to(send, (2,) + send.shape[1:])
    send = send.reshape(group_count * rank_count, slots, 2 * width)
    held = lax.all_to_all(send, both, split_axis=0, concat_axis=0, tiled=True)
    held = held.reshape(group_count, rank_count, slots, 2, width)
    held = held.transpose(3, 0, 2, 1, 4).reshape(2, group_count * slots, rank_count * width)
    gate_pre = times_rows(held[0], gate_weight[0])
    up_pre = times_rows(held[0], up_weight[0])
    back_proj = times_rows(held[1], down_weight[0])
    product, grad_gate_pre, grad_up_pre = gradients(gate_pre, up_pre, back_proj)
    inner_sum = jnp.sum(product, axis=1, keepdims=True)
    partial = times_units(grad_gate_pre, gate_weight[0]) + times_units(grad_up_pre, up_weight[0])
    back = partial.astype(jnp.bfloat16).reshape(group_count, slots, rank_count, width)
    back = back.transpose(0, 2, 1, 3)
    parts = jnp.concatenate(split_float(inner_sum), axis=1).astype(jnp.bfloat16)
    parts = jnp.pad(parts, ((0, 0), (0, extra - PARTS))).reshape(group_count, 1, slots, extra)
    parts = jnp.broadcast_to(parts, (group_count, rank_count, slots, extra))
    back = jnp.concatenate([back, parts], axis=-1)
    back = back.reshape(group_count * rank_count, slots, width + extra)
    arrived = lax.all_to_all(back, both, split_axis=0, concat_axis=0, tiled=True)
    arrived = arrived.reshape(2, pair_count * cap, width + extra).astype(jnp.float32)
    per_route = (arrived[0] + arrived[1])[slot_index].reshape(group_tokens, TOP, width + extra)
    grad_tokens = jnp.sum(per_route[..., :width] * route_weights[:, :, None], axis=1)
    grad_gates = jnp.sum(per_route[..., width : width + PARTS], axis=2)
    return (grad_tokens.astype(jnp.bfloat16), grad_gates)


def solution(mesh):
    groups, ranks = mesh.shape["grp"], mesh.shape["ep"]

    def run(tokens, *others):
        everywhere = groups == 2 * TOP and tokens.shape[0] == groups * LANES and ranks == 8
        if everywhere:
            fine = Mesh(mesh.devices.reshape([2] * 5), GROUP_AXES + RANK_AXES)
            placed, body, axes, grp = fine, every_expert, RANK_AXES, GROUP_AXES
        else:
            placed, body, axes, grp = mesh, by_slots, "ep", "grp"
        weights = [P(grp, None, None)] * 3
        return jax.shard_map(
            body,
            mesh=placed,
            in_specs=(P(grp, axes), P(grp, axes), P(grp, None), P(grp, None), *weights),
            out_specs=(P(grp, axes), P(grp, None)),
            check_vma=False,
        )(tokens, *others)

    return run
```

```python
import functools
import math

import jax
import jax.numpy as jnp
import numpy as np
from jax import lax
from jax.experimental import pallas as pl
from jax.experimental.pallas import tpu as pltpu
from jax.sharding import Mesh
from jax.sharding import PartitionSpec as P

TOP = 2
LANES = 128
PARTS = 2
TILE = 256
RANK_AXES = ("ep_y", "ep_x", "ep_core")
GROUP_AXES = ("grp_hi", "grp_lo")
SEND_AXES = ("ep_x", "ep_y", "grp_hi", "ep_core", "grp_lo")
VMEM_BYTES = 40 * 1024 * 1024


def gradients(gate_pre, up_pre, back_proj):
    sigmoid_gate = jax.nn.sigmoid(gate_pre)
    active = gate_pre * sigmoid_gate
    hidden = (active * up_pre).astype(jnp.bfloat16)
    product = hidden.astype(jnp.float32) * back_proj
    grad_gate_pre = back_proj * up_pre * sigmoid_gate * (1.0 + gate_pre * (1.0 - sigmoid_gate))
    grad_up_pre = back_proj * active
    return product, grad_gate_pre.astype(jnp.bfloat16), grad_up_pre.astype(jnp.bfloat16)


def times_rows(rows, weight):
    contract = (((1,), (1,)), ((), ()))
    return lax.dot_general(rows, weight, contract, preferred_element_type=jnp.float32)


def times_units(grads, weight):
    return jnp.dot(grads, weight, preferred_element_type=jnp.float32)


def split_float(value):
    first = value.astype(jnp.bfloat16).astype(jnp.float32)
    second = (value - first).astype(jnp.bfloat16).astype(jnp.float32)
    return first, second


def repeat_lanes(row, start, count):
    lane = lax.broadcasted_iota(jnp.int32, row.shape, 1)
    row = jnp.where((lane >= start) & (lane < start + count), row, 0.0)
    row = pltpu.roll(row, (LANES - start) % LANES, 1)
    while count < LANES:
        row = row + pltpu.roll(row, count, 1)
        count *= 2
    return row


def pack_kernel(places, tokens_hbm, grad_hbm, out_ref, tokens_ref, grad_ref, arrived):
    _, slots, width = out_ref.shape
    lanes = (slice(0, width // 2), slice(width // 2, width))
    copies = [
        pltpu.make_async_copy(tokens_hbm, tokens_ref, arrived.at[0]),
        pltpu.make_async_copy(grad_hbm, grad_ref, arrived.at[1]),
    ]
    for copy in copies:
        copy.start()
    for copy, source, half in zip(copies, (tokens_ref, grad_ref), lanes):
        copy.wait()
        for of_group in places:
            for rank, place in enumerate(of_group):
                out_ref[place, :, half] = source[rank * slots : (rank + 1) * slots, :]


def half_kernel(places, rows_ref, gate_ref, up_ref, down_ref, routes_ref, weights_ref, out_ref, scales_ref):
    group_count, rank_count = len(places), len(places[0])
    _, slots, width = rows_ref.shape
    width = width // 2
    total = group_count * slots
    slices = [slice(rank * width, (rank + 1) * width) for rank in range(rank_count)]
    units = gate_ref.shape[1]
    cut = units // TILE * TILE
    main, rest = slice(0, cut), slice(cut, units)

    gate_main = up_main = both_rest = turned = 0.0
    for at in range(0, rank_count * width, TILE):
        rank, start = divmod(at, width)
        columns = slice(at, at + TILE)
        first, second = slice(start, start + TILE), slice(width + start, width + start + TILE)
        rows_in = jnp.concatenate([rows_ref[of_group[rank], :, first] for of_group in places], axis=0)
        rows_back = jnp.concatenate([rows_ref[of_group[rank], :, second] for of_group in places], axis=0)
        both = jnp.concatenate([gate_ref[0, rest, columns], up_ref[0, rest, columns]], axis=0)
        gate_main = gate_main + times_rows(rows_in, gate_ref[0, main, columns])
        turned = turned + times_rows(down_ref[0, :, columns], rows_back)
        up_main = up_main + times_rows(rows_in, up_ref[0, main, columns])
        both_rest = both_rest + times_rows(rows_in, both)
    back_proj = jnp.concatenate([turned, jnp.zeros((units, LANES - total), jnp.float32)], axis=1).T[:total]
    back_main, back_rest = back_proj[:, main], back_proj[:, rest]
    product_main, by_gate_main, by_up_main = gradients(gate_main, up_main, back_main)
    product_rest, by_gate_rest, by_up_rest = gradients(
        both_rest[:, : units - cut], both_rest[:, units - cut :], back_rest
    )
    product = jnp.concatenate([product_main, product_rest], axis=1)
    by_rest = jnp.concatenate([by_gate_rest, by_up_rest], axis=1)

    taken = routes_ref[:1, :] == 0
    for expert, (one, other) in enumerate(((0, 1), (1, 0))):
        factor = jnp.where(taken, weights_ref[one : one + 1, :], weights_ref[other : other + 1, :])
        scales_ref[expert] = jnp.broadcast_to(factor, (LANES, LANES)).T

    folded = product[:, :LANES]
    for start in range(LANES, product.shape[1], LANES):
        folded = folded + product[:, start : start + LANES]
    folded = jnp.concatenate([folded, jnp.zeros((LANES - total, LANES), jnp.float32)], axis=0)
    inner_sum = jnp.sum(folded.T, axis=0, keepdims=True)
    line = lax.broadcasted_iota(jnp.int32, (2, LANES), 0)
    for group in range(group_count):
        tail = jnp.zeros((2, LANES), jnp.float32)
        for index, piece in enumerate(split_float(repeat_lanes(inner_sum, group * slots, slots))):
            tail = jnp.where(line == index, piece, tail)
        for place in places[group]:
            out_ref[place, slots * (width // LANES) // 2] = tail.astype(jnp.bfloat16)

    for rank, columns in enumerate(slices):
        weight_rest = jnp.concatenate([gate_ref[0, rest, columns], up_ref[0, rest, columns]], axis=0)
        partial = times_units(by_gate_main, gate_ref[0, main, columns])
        partial = partial + times_units(by_up_main, up_ref[0, main, columns])
        partial = partial + times_units(by_rest, weight_rest)
        partial = partial.astype(jnp.bfloat16)
        for group in range(group_count):
            rows = slice(group * slots, (group + 1) * slots)
            for index in range(width // LANES):
                lanes = slice(index * LANES, (index + 1) * LANES)
                pairs = slice(index * slots // 2, (index + 1) * slots // 2)
                out_ref[places[group][rank], pairs] = partial[rows, lanes].reshape(slots // 2, 2, LANES)


def owner_kernel(places, parts_ref, routes_ref, scales_ref, grad_ref, gates_ref):
    count, length, _, _ = parts_ref.shape
    total, width = grad_ref.shape
    slots = total // len(places[0])
    body = slots * (width // LANES) // 2
    for rank in range(len(places[0])):
        rows = slice(rank * slots, (rank + 1) * slots)
        for index in range(width // LANES):
            pairs = slice(index * slots // 2, (index + 1) * slots // 2)
            value = 0.0
            for expert in range(TOP):
                pair = parts_ref[places[expert][rank], pairs].astype(jnp.float32)
                pair = pair + parts_ref[places[expert + TOP][rank], pairs].astype(jnp.float32)
                value = value + scales_ref[expert, rows, :] * pair.reshape(slots, LANES)
            grad_ref[rows, index * LANES : (index + 1) * LANES] = value.astype(jnp.bfloat16)
    owner = lax.broadcasted_iota(jnp.int32, (2, LANES), 1) // slots
    inner = []
    for expert in range(TOP):
        value = jnp.zeros((2, LANES), jnp.float32)
        for rank in range(len(places[0])):
            pair = parts_ref[places[expert][rank], body].astype(jnp.float32)
            pair = pair + parts_ref[places[expert + TOP][rank], body].astype(jnp.float32)
            value = value + jnp.where(owner == rank, pair, 0.0)
        inner.append(jnp.sum(value, axis=0, keepdims=True))
    gates_ref[...] = jnp.where(routes_ref[...] == 0, inner[0], inner[1])


def message_places(order):
    axes = GROUP_AXES + RANK_AXES
    sizes = [lax.axis_size(axis) for axis in axes]
    linear = np.arange(math.prod(sizes)).reshape([lax.axis_size(axis) for axis in order])
    linear = linear.transpose([order.index(axis) for axis in axes])
    return linear.reshape(sizes[0] * sizes[1], -1).tolist()


def every_expert(tokens, grad_out, routes, route_weights, gate_weight, up_weight, down_weight):
    rank_count = lax.axis_size(RANK_AXES)
    count = lax.axis_size(SEND_AXES)
    group_tokens, width = tokens.shape
    slots = group_tokens // rank_count
    length = slots * (width // LANES) // 2 + 1
    whole = pl.BlockSpec(memory_space=pltpu.VMEM)
    there = pl.BlockSpec(memory_space=pltpu.HBM)
    params = pltpu.CompilerParams(vmem_limit_bytes=VMEM_BYTES)
    places = message_places(SEND_AXES)

    send = pl.pallas_call(
        functools.partial(pack_kernel, places),
        out_shape=jax.ShapeDtypeStruct((count, slots, 2 * width), tokens.dtype),
        in_specs=[there] * 2,
        out_specs=whole,
        scratch_shapes=[
            pltpu.VMEM(tokens.shape, tokens.dtype),
            pltpu.VMEM(tokens.shape, tokens.dtype),
            pltpu.SemaphoreType.DMA((2,)),
        ],
        compiler_params=params,
    )(*[pltpu.with_memory_space_constraint(value, pltpu.HBM) for value in (tokens, grad_out)])
    send, up_weight, down_weight = lax.optimization_barrier((send, up_weight, down_weight))
    up_weight = lax.ppermute(up_weight, RANK_AXES[-1], [(0, 1), (1, 0)])
    down_weight = lax.ppermute(down_weight, RANK_AXES[-1], [(0, 1), (1, 0)])
    held = lax.all_to_all(send, SEND_AXES, split_axis=0, concat_axis=0, tiled=True)
    back, scales = pl.pallas_call(
        functools.partial(half_kernel, places),
        out_shape=(
            jax.ShapeDtypeStruct((count, length, 2, LANES), jnp.bfloat16),
            jax.ShapeDtypeStruct((TOP, group_tokens, LANES), jnp.float32),
        ),
        in_specs=[whole] * 6,
        out_specs=(whole, whole),
        compiler_params=params,
    )(
        held,
        gate_weight,
        up_weight,
        down_weight,
        routes.T,
        route_weights.T,
    )
    arrived = lax.all_to_all(back, SEND_AXES, split_axis=0, concat_axis=0, tiled=True)
    grad_tokens, grad_gates = pl.pallas_call(
        functools.partial(owner_kernel, places),
        out_shape=(
            jax.ShapeDtypeStruct(tokens.shape, jnp.bfloat16),
            jax.ShapeDtypeStruct((TOP, group_tokens), jnp.float32),
        ),
        in_specs=[whole] * 3,
        out_specs=(whole, whole),
        compiler_params=params,
    )(arrived, routes.T, scales)
    return grad_tokens, grad_gates.T


def slot_tables(routes, pair_count, cap):
    flat_expert = routes.reshape(-1)
    route_total = flat_expert.shape[0]
    onehot = (flat_expert[:, None] == jnp.arange(pair_count, dtype=jnp.int32)[None, :]).astype(
        jnp.int32
    )
    running = jnp.cumsum(onehot, axis=0)
    slot_index = flat_expert * cap + jnp.sum((running - 1) * onehot, axis=1)
    slot_total = pair_count * cap
    source_token = (
        jnp.zeros((slot_total,), jnp.int32)
        .at[slot_index]
        .set(jnp.arange(route_total, dtype=jnp.int32) // TOP)
    )
    filled = jnp.zeros((slot_total,), jnp.bool_).at[slot_index].set(True)
    return slot_index, source_token, filled


def by_slots(tokens, grad_out, routes, route_weights, gate_weight, up_weight, down_weight):
    group_count = lax.axis_size("grp")
    rank_count = lax.axis_size("ep")
    pair_count = group_count // 2
    both = ("grp", "ep")
    group_tokens, width = tokens.shape
    per_device = group_tokens // rank_count
    slots = 2 * ((per_device * TOP + 2 * pair_count - 1) // (2 * pair_count))
    cap = rank_count * slots
    extra = LANES
    slot_index, source_token, filled = slot_tables(routes, pair_count, cap)

    paired = jnp.concatenate([tokens, grad_out], axis=1)
    packed = jnp.where(filled[:, None], paired[source_token], jnp.zeros((), paired.dtype))
    send = packed.reshape(1, pair_count, rank_count, slots, 2 * width)
    send = jnp.broadcast_to(send, (2,) + send.shape[1:])
    send = send.reshape(group_count * rank_count, slots, 2 * width)
    held = lax.all_to_all(send, both, split_axis=0, concat_axis=0, tiled=True)
    held = held.reshape(group_count, rank_count, slots, 2, width)
    held = held.transpose(3, 0, 2, 1, 4).reshape(2, group_count * slots, rank_count * width)
    gate_pre = times_rows(held[0], gate_weight[0])
    up_pre = times_rows(held[0], up_weight[0])
    back_proj = times_rows(held[1], down_weight[0])
    product, grad_gate_pre, grad_up_pre = gradients(gate_pre, up_pre, back_proj)
    inner_sum = jnp.sum(product, axis=1, keepdims=True)
    partial = times_units(grad_gate_pre, gate_weight[0]) + times_units(grad_up_pre, up_weight[0])
    back = partial.astype(jnp.bfloat16).reshape(group_count, slots, rank_count, width)
    back = back.transpose(0, 2, 1, 3)
    parts = jnp.concatenate(split_float(inner_sum), axis=1).astype(jnp.bfloat16)
    parts = jnp.pad(parts, ((0, 0), (0, extra - PARTS))).reshape(group_count, 1, slots, extra)
    parts = jnp.broadcast_to(parts, (group_count, rank_count, slots, extra))
    back = jnp.concatenate([back, parts], axis=-1)
    back = back.reshape(group_count * rank_count, slots, width + extra)
    arrived = lax.all_to_all(back, both, split_axis=0, concat_axis=0, tiled=True)
    arrived = arrived.reshape(2, pair_count * cap, width + extra).astype(jnp.float32)
    per_route = (arrived[0] + arrived[1])[slot_index].reshape(group_tokens, TOP, width + extra)
    grad_tokens = jnp.sum(per_route[..., :width] * route_weights[:, :, None], axis=1)
    grad_gates = jnp.sum(per_route[..., width : width + PARTS], axis=2)
    return (grad_tokens.astype(jnp.bfloat16), grad_gates)


def solution(mesh):
    groups, ranks = mesh.shape["grp"], mesh.shape["ep"]

    def run(tokens, *others):
        everywhere = groups == 2 * TOP and tokens.shape[0] == groups * LANES and ranks == 8
        if everywhere:
            fine = Mesh(mesh.devices.reshape([2] * 5), GROUP_AXES + RANK_AXES)
            placed, body, axes, grp = fine, every_expert, RANK_AXES, GROUP_AXES
        else:
            placed, body, axes, grp = mesh, by_slots, "ep", "grp"
        weights = [P(grp, None, None)] * 3
        return jax.shard_map(
            body,
            mesh=placed,
            in_specs=(P(grp, axes), P(grp, axes), P(grp, None), P(grp, None), *weights),
            out_specs=(P(grp, axes), P(grp, None)),
            check_vma=False,
        )(tokens, *others)

    return run
```
